32 devices in a mesh: step: 8 (over y, x, core), tile: 4 (over z).
Axes of the slice: x: 2, y: 2, z: 4, core: 2. Of those that a mesh axis runs over, the one named last changes fastest.
Arguments:
- target_left: float32 [16, 4, 2048, 128], P('step', 'tile'), may hold values from -6 to 6
- target_right: float32 [16, 4, 2048, 128], P('step', 'tile'), may hold values from -0.125 to 0.125
- column_left: float32 [16, 2048, 128], P('step', 'tile'), may hold values from -12 to 12
- column_right: float32 [16, 2048, 128], P('step', 'tile'), may hold values from -0.125 to 0.125
- sketch: float32 [2048, 128], P('tile'), may hold values from -6 to 6
- pattern: int32 [16, 4], P('step', 'tile'), may hold values from 0 to 1, as said below
Outputs:
- basis: float32 [4, 2048, 128], P('tile', 'step')
- factor: float32 [4, 2048, 128], P('tile', 'step')
The draws below stay inside these ranges and needn't reach their ends.
Inputs may be any that keep to these rules, and one draw needn't show every extreme that they name: `pattern`: every target has at least 8 existing products; some target has exactly that many and some target has all 16.
All inputs are finite; a program needn't handle non-finite values.
Results may differ from the reference program's by a relative error of at most 0.00023.
Values sent between devices are 32-bit elements; how exact they have to be, the bound alone decides.
No kernel may reach another device: no remote copies, remote signals or barrier semaphores. Data moves between devices by JAX's collectives and lax.ppermute only.
A program may use at most 64 MiB of HBM per device.

```python
import jax
import jax.numpy as jnp
from jax import lax

TILE = 2048
RANK = 128
STEPS = 16
TARGETS = 4


def draw_pattern(key, part):
    keys = jax.random.split(jax.random.fold_in(key, 17), 4)
    counts = jax.random.randint(keys[0], (TARGETS,), STEPS // 2, STEPS + 1)
    first = jax.random.randint(keys[1], (), 0, TARGETS)
    second = (first + 1 + jax.random.randint(keys[2], (), 0, TARGETS - 1)) % TARGETS
    places = jnp.arange(TARGETS)
    counts = jnp.where(places == first, STEPS // 2, counts)
    counts = jnp.where(places == second, STEPS, counts)
    ranking = jax.vmap(lambda sub: jax.random.permutation(sub, STEPS))(jax.random.split(keys[3], TARGETS))
    return (ranking < counts[:, None]).T.astype(jnp.int32)


def level_of(key, shape, pieces, least, top_value):
    factor_of, own = 1.0, jax.random.fold_in(key, 6)
    for dim, blocks in pieces:
        draws = jnp.exp(jax.random.uniform(jax.random.fold_in(own, dim), (blocks,), jnp.float32, least / len(pieces), top_value / len(pieces)))
        factor_of = factor_of * jnp.repeat(draws, shape[dim] // blocks).reshape([-1 if axis == dim else 1 for axis in range(len(shape))])
    return factor_of


def centred(own_key, dims, spread, limit, pieces=(), kind=jnp.bfloat16):
    values = jax.random.normal(own_key, dims, jnp.float32) * spread
    if len(pieces) > 0:
        values = level_of(own_key, dims, pieces, -0.22, 0.18) * values
    return jnp.clip(values, min=-limit, max=limit).astype(kind)


def setup_inputs(seed: int = 0) -> dict:
    splits = jax.random.split(jax.random.key(seed), 7)
    target_left = centred(splits[0], (STEPS, TARGETS, TILE, RANK), 1.0, 6.0, ((0, 8), (1, 4)), jnp.float32)
    target_right = centred(splits[1], (STEPS, TARGETS, TILE, RANK), TILE ** -0.5, 0.125, ((0, 8), (1, 4)), jnp.float32)
    column_left = centred(splits[2], (STEPS, TILE, RANK), 2.0, 12.0, ((0, 8), (1, 4)), jnp.float32)
    column_right = centred(splits[3], (STEPS, TILE, RANK), TILE ** -0.5, 0.125, ((0, 8), (1, 4)), jnp.float32)
    sketch = centred(splits[4], (TILE, RANK), 1.0, 6.0, ((0, 4),), jnp.float32)
    pattern = draw_pattern(jax.random.fold_in(splits[6], 71), 0)
    return dict(target_left=target_left, target_right=target_right, column_left=column_left, column_right=column_right, sketch=sketch, pattern=pattern)


def orthonormal(sketched):
    highest = lax.Precision.HIGHEST
    gram_matrix = jnp.dot(sketched.T.astype(jnp.float32), sketched.astype(jnp.float32), precision=highest, preferred_element_type=jnp.float32) / TILE
    lower_factor = jnp.linalg.cholesky(gram_matrix)
    return jax.scipy.linalg.solve_triangular(lower_factor, sketched.T, lower=True).T

def reference(target_left, target_right, column_left, column_right, sketch, pattern):
    highest = lax.Precision.HIGHEST
    weights = pattern.astype(jnp.float32)
    probes = jnp.einsum('kbq,bp->kqp', column_left, sketch, precision=highest)

    def per_target(target):
        left_tile = lax.dynamic_index_in_dim(target_left, target, 1, keepdims=False)
        right_tile = lax.dynamic_index_in_dim(target_right, target, 1, keepdims=False)
        present = lax.dynamic_index_in_dim(weights, target, 1, keepdims=False)
        core_tile = jnp.einsum('kbr,kbq->krq', right_tile, column_right, precision=highest) * present[:, None, None]
        reduced = jnp.einsum('krq,kqp->krp', core_tile, probes, precision=highest)
        sketched = jnp.einsum('kbr,krp->bp', left_tile, reduced, precision=highest)
        basis_full = orthonormal(sketched)
        projected = jnp.einsum('kbr,bp->krp', left_tile, basis_full, precision=highest)
        returned = jnp.einsum('krq,krp->kqp', core_tile, projected, precision=highest)
        factor_full = jnp.einsum('kbq,kqp->bp', column_left, returned, precision=highest) / TILE
        return (basis_full, factor_full)
    bases, factors = lax.map(per_target, jnp.arange(TARGETS, dtype=jnp.int32))
    return (bases, factors)
```

```python
import jax
import jax.numpy as jnp
from jax import lax
from jax.sharding import PartitionSpec as P

HIGH = lax.Precision.HIGH


def mm(spec, *arrays):
    return jnp.einsum(spec, *arrays, precision=HIGH, preferred_element_type=jnp.float32)


def inverse_factor(gram):
    lower = jnp.linalg.cholesky(gram)
    eye = jnp.eye(gram.shape[-1], dtype=gram.dtype)
    return jax.scipy.linalg.solve_triangular(lower, eye, lower=True)


def exchange(array, axis, bit):
    return lax.ppermute(array, axis, [(i, i ^ bit) for i in range(lax.axis_size(axis))])


def take(array, index, axis):
    return lax.dynamic_index_in_dim(array, index, axis, keepdims=False)


def local_general(target_left, target_right, column_left, column_right, sketch, pattern):
    left, right = target_left[:, 0], target_right[:, 0]
    tile_rows = left.shape[1]
    probes = lax.psum(mm("kbq,bp->kqp", column_left, sketch), "tile")
    col_left = lax.all_gather(column_left, "tile", axis=1, tiled=True)
    col_right = lax.all_gather(column_right, "tile", axis=1, tiled=True)
    core = mm("kbr,kbq->krq", right, col_right) * pattern[:, 0].astype(jnp.float32)[:, None, None]
    reduced = mm("krq,kqp->krp", core, probes)
    sketched = lax.psum(mm("kbr,krp->bp", left, reduced), "step")
    inverse = inverse_factor(mm("bp,bq->pq", sketched, sketched) / tile_rows)
    row_count = tile_rows // lax.axis_size("step")
    rows = lax.dynamic_slice_in_dim(sketched, lax.axis_index("step") * row_count, row_count, 0)
    projected = mm("kbr,bp->krp", left, sketched)
    returned = mm("krq,krp->kqp", core, projected)
    partial = mm("kbq,kqp->bp", col_left, returned)
    factor = lax.psum_scatter(partial, "step", scatter_dimension=0, tiled=True) / tile_rows
    return mm("bp,qp->bq", rows, inverse)[None], mm("bp,qp->bq", factor, inverse)[None]


def local_line(target_left, target_right, column_left, column_right, sketch, pattern):
    left, right = target_left[:, 0], target_right[:, 0]
    tile_rows, rank = left.shape[1:]
    planes = lax.axis_size("tile")
    chips = lax.axis_size("step") // 2
    plane = lax.axis_index("tile")
    core_bit = lax.axis_index("step") % 2
    chip = lax.axis_index("step") // 2
    row_count = tile_rows // (2 * chips)
    up, down = [(0, 1), (1, 2), (2, 3)], [(1, 0), (2, 1), (3, 2)]
    inner_up, inner_down = [(1, 2), (2, 3)], [(2, 1), (1, 0)]

    def across(array, pairs):
        return lax.ppermute(array, "tile", pairs)

    from_below = across(column_right, up)
    from_above = across(column_right, down)
    right_blocks = right.reshape(2, planes, -1, rank)
    lent = across(take(right_blocks, jnp.where(plane == 0, planes - 1, 0), 1), [(0, 1), (3, 2)])
    probes = mm("kbq,bp->kqp", column_left, sketch)
    probes = probes + exchange(probes, "tile", 1)
    probes = probes + exchange(probes, "tile", 2)
    far = across(from_below, inner_up) + across(from_above, inner_down)
    far_index = jnp.where(plane < 2, plane + 2, plane - 2)

    def block(index):
        return take(right_blocks, index, 1)

    core = (
        mm("kbr,kbq->krq", block(plane), column_right)
        + mm("kbr,kbq->krq", block(jnp.maximum(plane - 1, 0)), from_below)
        + mm("kbr,kbq->krq", block(jnp.minimum(plane + 1, planes - 1)), from_above)
    )
    core = core + mm("kbr,kbq->krq", block(far_index), far)
    core = core + across(mm("kbr,kbq->krq", lent, far), [(1, 0), (2, 3)])
    core = core * pattern[:, 0].astype(jnp.float32)[:, None, None]
    left_split = left.reshape(2, chips, 2, row_count, rank)
    left_mine = take(left_split, core_bit, 2)
    left_other = exchange(take(left_split, 1 - core_bit, 2), "step", 1)
    col_split = column_left.reshape(2, 2, row_count, rank)
    col_half = jnp.concatenate([take(col_split, core_bit, 1), exchange(take(col_split, 1 - core_bit, 1), "step", 1)])
    col_below = across(col_half, up)
    col_above = across(col_half, down)
    col_far = across(col_below, inner_up) + across(col_above, inner_down)
    col_last = across(col_far, [(1, 0), (2, 3)])

    both = jnp.concatenate([mm("krq,kqp->krp", core, probes), core])
    both_other = exchange(both, "step", 1)
    core_other = both_other[2:]
    y_part = mm("kcbr,krp->cbp", left_mine, both[:2]) + mm("kcbr,krp->cbp", left_other, both_other[:2])

    def scatter(parts):
        total = take(parts, chip, 0)
        for bit in range(1, chips):
            total = total + exchange(take(parts, chip ^ bit, 0), "step", 2 * bit)
        return total

    y_rows = scatter(y_part)
    y_all = jnp.stack([y_rows] + [exchange(y_rows, "step", 2 * bit) for bit in range(1, chips)])
    order = chip ^ jnp.arange(chips)

    def z_of(part):
        return sum(mm("kbr,bp->krp", take(part, order[i], 1), y_all[i]) for i in range(chips))

    z_mine, z_other = z_of(left_mine), z_of(left_other)
    gram = mm("cbp,cbq->pq", y_all, y_all)[None]
    summed = jnp.concatenate([z_mine, z_other, gram]) + exchange(jnp.concatenate([z_other, z_mine, gram]), "step", 1)
    n_all = mm("krq,krp->kqp", jnp.concatenate([core, core_other]), summed[:4])
    w_mine = mm("kbq,kqp->bp", col_half, n_all)
    w_below = mm("kbq,kqp->bp", col_below, n_all)
    w_above = mm("kbq,kqp->bp", col_above, n_all)
    w_far = mm("kbq,kqp->bp", col_far, n_all)
    w_last = mm("kbq,kqp->bp", col_last, n_all)

    def w_block(index):
        distance = index - plane
        return jnp.where(
            distance == 0, w_mine,
            jnp.where(distance == 1, w_above,
                      jnp.where(distance == -1, w_below,
                                jnp.where(jnp.abs(distance) == 2, w_far, w_last))),
        )

    w_part = jnp.stack([w_block(i) for i in range(planes)])
    w_rows = scatter(w_part) / tile_rows
    inverse = inverse_factor(summed[4] / tile_rows)
    return mm("bp,qp->bq", y_rows, inverse)[None], mm("bp,qp->bq", w_rows, inverse)[None]


def solution(mesh):
    line = mesh.shape["tile"] == 4 and mesh.shape["step"] == 8
    return jax.shard_map(
        local_line if line else local_general,
        mesh=mesh,
        in_specs=(
            P("step", "tile", None, None),
            P("step", "tile", None, None),
            P("step", "tile", None),
            P("step", "tile", None),
            P("tile", None),
            P("step", "tile"),
        ),
        out_specs=(P("tile", "step", None), P("tile", "step", None)),
        check_vma=False,
    )
```

```python
import functools

import jax
import jax.numpy as jnp
from jax import lax
from jax.experimental import pallas as pl
from jax.experimental.pallas import tpu as pltpu
from jax.sharding import PartitionSpec as P

HIGH = lax.Precision.HIGH


def mm(spec, *arrays):
    return jnp.einsum(spec, *arrays, precision=HIGH, preferred_element_type=jnp.float32)


def inverse_factor(gram):
    lower = jnp.linalg.cholesky(gram)
    eye = jnp.eye(gram.shape[-1], dtype=gram.dtype)
    return jax.scipy.linalg.solve_triangular(lower, eye, lower=True)


def exchange(array, axis, bit):
    return lax.ppermute(array, axis, [(i, i ^ bit) for i in range(lax.axis_size(axis))])


def take(array, index, axis):
    return lax.dynamic_index_in_dim(array, index, axis, keepdims=False)


def local_general(target_left, target_right, column_left, column_right, sketch, pattern):
    left, right = target_left[:, 0], target_right[:, 0]
    tile_rows = left.shape[1]
    probes = lax.psum(mm("kbq,bp->kqp", column_left, sketch), "tile")
    col_left = lax.all_gather(column_left, "tile", axis=1, tiled=True)
    col_right = lax.all_gather(column_right, "tile", axis=1, tiled=True)
    core = mm("kbr,kbq->krq", right, col_right) * pattern[:, 0].astype(jnp.float32)[:, None, None]
    reduced = mm("krq,kqp->krp", core, probes)
    sketched = lax.psum(mm("kbr,krp->bp", left, reduced), "step")
    inverse = inverse_factor(mm("bp,bq->pq", sketched, sketched) / tile_rows)
    row_count = tile_rows // lax.axis_size("step")
    rows = lax.dynamic_slice_in_dim(sketched, lax.axis_index("step") * row_count, row_count, 0)
    projected = mm("kbr,bp->krp", left, sketched)
    returned = mm("krq,krp->kqp", core, projected)
    partial = mm("kbq,kqp->bp", col_left, returned)
    factor = lax.psum_scatter(partial, "step", scatter_dimension=0, tiled=True) / tile_rows
    return mm("bp,qp->bq", rows, inverse)[None], mm("bp,qp->bq", factor, inverse)[None]


TN = (((0,), (0,)), ((), ()))
NN = (((1,), (0,)), ((), ()))
NT = (((1,), (1,)), ((), ()))


def split(array):
    high = array.astype(jnp.bfloat16)
    return high, (array - high.astype(jnp.float32)).astype(jnp.bfloat16)


def dot3(a, b, dims):
    a_high, a_low = split(a)
    b_high, b_low = split(b)
    axis = 1 - dims[0][1][0]
    width = b.shape[axis]
    dot = functools.partial(lax.dot_general, dimension_numbers=dims, preferred_element_type=jnp.float32)
    wide = dot(a_high, jnp.concatenate([b_high, b_low], axis))
    return wide[:, :width] + wide[:, width:] + dot(a_low, b_high)


def dot_full(a, b, dims):
    return lax.dot_general(a, b, dims, precision=lax.Precision.HIGHEST, preferred_element_type=jnp.float32)


def call(kernel, outs, args, spaces="", scratch=(), cost=0):
    kinds = {"v": pltpu.VMEM, "a": pl.ANY, "s": pltpu.SMEM}
    spaces = spaces or "v" * len(args)
    shapes = [jax.ShapeDtypeStruct(shape, jnp.float32) for shape in outs]
    return pl.pallas_call(
        kernel,
        out_shape=shapes,
        in_specs=[pl.BlockSpec(memory_space=kinds[letter]) for letter in spaces],
        out_specs=[pl.BlockSpec(memory_space=pltpu.VMEM) for _ in shapes],
        scratch_shapes=list(scratch),
        compiler_params=pltpu.CompilerParams(vmem_limit_bytes=24 << 20),
        cost_estimate=pl.CostEstimate(flops=cost, bytes_accessed=1 << 20, transcendentals=0),
    )(*args)


def core_kernel(planes, part, own_rows, first, second, core, lent):
    plane = lax.axis_index("tile")
    is_end = jnp.logical_or(plane == 0, plane == planes - 1)

    @pl.when(is_end)
    def _():
        for k in range(2):
            core[k] = part[k] + dot3(own_rows[k], second[k], TN)
            lent[k] = jnp.zeros_like(lent[k])

    @pl.when(jnp.logical_not(is_end))
    def _():
        for k in range(2):
            core[k] = part[k] + dot3(own_rows[k], first[k], TN)
            lent[k] = dot3(second[k], first[k], TN)


def reduced_kernel(core, lent, probe_here, probe_far, pattern, both):
    for k in range(2):
        weight = pattern[k, 0].astype(jnp.float32)
        c = (core[k] + lent[k]) * weight
        both[k] = dot3(c, probe_here[k] + probe_far[k] + lent[2 + k], NN)
        both[2 + k] = c


def start_rows(left, left_other, held, sems, chips, rows):
    position = lax.axis_index("step")
    chip, bit = position // 2, position % 2
    copies = []
    for i in range(chips):
        block = jnp.bitwise_xor(chip, i)
        mine = left.at[:, 0, pl.ds(pl.multiple_of((block * 2 + bit) * rows, rows), rows), :]
        copies.append((
            pltpu.make_async_copy(mine, held.at[i, pl.ds(0, 2)], sems.at[2 * i]),
            pltpu.make_async_copy(left_other.at[:, block], held.at[i, pl.ds(2, 2)], sems.at[2 * i + 1]),
        ))
    for pair in copies:
        for copy in pair:
            copy.start()
    return copies


def y_kernel(left, left_other, both, both_other, *rest):
    *outs, held, sems = rest
    chips, rows = len(outs), outs[0].shape[0]
    copies = start_rows(left, left_other, held, sems, chips, rows)
    reduced = jnp.concatenate([both[0], both[1], both_other[0], both_other[1]], 0)
    for i, out in enumerate(outs):
        for copy in copies[i]:
            copy.wait()
        out[...] = dot3(jnp.concatenate([held[i, k] for k in range(4)], 1), reduced, NN)


def z_kernel(left, left_other, *rest):
    *ys, out, held, sems = rest
    chips, rows = len(ys), ys[0].shape[0]
    rank = out.shape[-1]
    copies = start_rows(left, left_other, held, sems, chips, rows)
    total = jnp.zeros((rank, 5 * rank), jnp.float32)
    dot = functools.partial(lax.dot_general, dimension_numbers=TN, preferred_element_type=jnp.float32)
    for i, y in enumerate(ys):
        y_here = y[...]
        for copy in copies[i]:
            copy.wait()
        beside = jnp.concatenate([held[i, 2], held[i, 3], held[i, 0], held[i, 1], y_here], 1)
        b_high, b_low = split(beside)
        a_high, a_low = split(y_here)
        total += dot(a_high, b_high) + dot(a_high, b_low) + dot(a_low, b_high)
    for k in range(5):
        out[k] = total[:, k * rank:(k + 1) * rank]


def w_kernel(planes, sent, got, both, both_other, own, near, inner, inner_far, outer, last, *rest):
    *outs, gram, held, sems = rest
    plane = lax.axis_index("tile")
    chip = lax.axis_index("step") // 2
    is_end = jnp.logical_or(plane == 0, plane == planes - 1)

    def pick(i, wanted, source):
        @pl.when(wanted)
        def _():
            pltpu.make_async_copy(source, held.at[i], sems.at[i]).start()

    for i in range(planes):
        block = jnp.bitwise_xor(chip, i)
        apart = jnp.bitwise_xor(block, plane)
        pick(i, apart == 0, own)
        pick(i, apart == 1, near)
        pick(i, jnp.logical_and(apart == 2, is_end), outer)
        pick(i, jnp.logical_and(apart == 2, jnp.logical_not(is_end)), inner_far)
        pick(i, jnp.logical_and(apart == 3, is_end), last)
        pick(i, jnp.logical_and(apart == 3, jnp.logical_not(is_end)), inner)
    gram[...] = sent[4] + got[4]
    returned = []
    for k in range(2):
        returned.append(dot3(sent[2 + k] + got[k], both[2 + k], NN))
    for k in range(2):
        returned.append(dot3(sent[k] + got[2 + k], both_other[2 + k], NN))
    returned = jnp.concatenate(returned, 1)
    for i, out in enumerate(outs):
        pltpu.make_async_copy(own, held.at[i], sems.at[i]).wait()
        out[...] = dot3(jnp.concatenate([held[i, k] for k in range(4)], 1), returned, NT)


def basis_kernel(tile_rows, width, gram, y_rows, basis, inverse):
    rank = gram.shape[0]
    scaled = gram[...] * (1.0 / tile_rows)
    eye = (lax.broadcasted_iota(jnp.int32, (rank, rank), 0) == lax.broadcasted_iota(jnp.int32, (rank, rank), 1))
    work = jnp.concatenate([scaled, eye.astype(jnp.float32)], 1)
    done = []
    for begin in range(0, rank, width):
        panel = work[:width]
        row_index = lax.broadcasted_iota(jnp.int32, (width, 1), 0)
        scale = jnp.zeros((width, 1), jnp.float32)
        for j in range(width):
            column = panel[:, begin + j:begin + j + 1]
            pivot = panel[j:j + 1, begin + j:begin + j + 1]
            factor = jnp.where(row_index > j, column * (1.0 / pivot), 0.0)
            scale = jnp.where(row_index == j, lax.rsqrt(pivot), scale)
            panel = panel - factor * panel[j:j + 1]
        panel = panel * scale
        done.append(panel[:, rank:])
        if begin + width < rank:
            work = work[width:] - dot_full(panel[:, begin + width:rank], panel, TN)
    lower_inverse = jnp.concatenate(done, 0)
    inverse[...] = lower_inverse
    basis[...] = dot_full(y_rows[...], lower_inverse, NT)


def factor_kernel(tile_rows, a, b, c, d, inverse, factor):
    total = (a[...] + b[...] + c[...] + d[...]) * (1.0 / tile_rows)
    factor[...] = dot_full(total, inverse[...], NT)


def local_line(target_left, target_right, column_left, column_right, sketch, pattern):
    tile_rows, rank = target_left.shape[2:]
    planes = lax.axis_size("tile")
    chips = lax.axis_size("step") // 2
    plane = lax.axis_index("tile")
    core_bit = lax.axis_index("step") % 2
    chip = lax.axis_index("step") // 2
    row_count = tile_rows // (2 * chips)
    is_end = jnp.logical_or(plane == 0, plane == planes - 1)
    outer_pairs, inner_pairs = [(0, 1), (1, 0), (2, 3), (3, 2)], [(1, 2), (2, 1)]
    outward = [(1, 0), (2, 3)]

    def across(array, pairs):
        return lax.ppermute(array, "tile", pairs)

    near = across(column_right, outer_pairs)
    inner = across(column_right, inner_pairs)
    probes = mm("kbq,bp->kqp", column_left, sketch)
    probes = probes + across(probes, outer_pairs)
    right_blocks = target_right.reshape(2, planes, -1, rank)

    def block(index):
        return take(right_blocks, index, 1)

    inner_far = across(near, inner_pairs)
    outer = across(jnp.where(is_end, block(planes - 1 - plane), inner), outer_pairs)
    probes_far = across(probes, inner_pairs)
    part = (
        mm("kbr,kbq->krq", block(plane), column_right)
        + mm("kbr,kbq->krq", block(plane ^ 1), near)
        + mm("kbr,kbq->krq", block(jnp.where(is_end, plane, planes - 1 - plane)), inner)
    )
    far_rows = block(plane ^ 2)
    core, lent = call(functools.partial(core_kernel, planes), [(2, rank, rank)] * 2, [part, far_rows, inner_far, outer])
    lent = across(jnp.concatenate([lent, probes_far]), outward)

    left_split = target_left.reshape(2, chips, 2, row_count, rank)
    left_other = exchange(take(left_split, 1 - core_bit, 2), "step", 1)
    col_split = column_left.reshape(2, 2, row_count, rank)
    col_half = jnp.concatenate([take(col_split, core_bit, 1), exchange(take(col_split, 1 - core_bit, 1), "step", 1)])
    col_half, _ = lax.optimization_barrier((col_half, near))
    col_near = across(col_half, outer_pairs)
    col_inner = across(col_half, inner_pairs)
    col_inner_far = across(col_near, inner_pairs)
    col_outer = across(col_inner, outward)
    col_last = across(col_inner_far, outward)

    (both,) = call(reduced_kernel, [(4, rank, rank)], [core, lent, probes, probes_far, pattern], "vvvvs")
    both_other = exchange(both, "step", 1)
    rows_scratch = [pltpu.VMEM((chips, 4, row_count, rank), jnp.float32), pltpu.SemaphoreType.DMA((2 * chips,))]
    y_parts = call(y_kernel, [(row_count, rank)] * chips, [target_left, left_other, both, both_other], "aavv", rows_scratch)
    y_rows = y_parts[0]
    for bit in range(1, chips):
        y_rows = y_rows + exchange(y_parts[bit], "step", 2 * bit)
    y_all = [y_rows] + [exchange(y_rows, "step", 2 * bit) for bit in range(1, chips)]
    (sent,) = call(z_kernel, [(5, rank, rank)], [target_left, left_other, *y_all], "aa" + "v" * chips, rows_scratch)
    got = exchange(sent, "step", 1)
    *w_parts, gram = call(
        functools.partial(w_kernel, planes),
        [(row_count, rank)] * planes + [(rank, rank)],
        [sent, got, both, both_other, col_half, col_near, col_inner, col_inner_far, col_outer, col_last],
        "vvvvaaaaaa",
        [pltpu.VMEM((planes, 4, row_count, rank), jnp.float32), pltpu.SemaphoreType.DMA((planes,))],
    )
    w_got = [exchange(w_parts[bit], "step", 2 * bit) for bit in range(1, chips)]
    basis, inverse = call(
        functools.partial(basis_kernel, tile_rows, 32), [(row_count, rank), (rank, rank)], [gram, y_rows], cost=10**9
    )
    (factor,) = call(functools.partial(factor_kernel, tile_rows), [(row_count, rank)], [w_parts[0], *w_got, inverse])
    return basis[None], factor[None]


def solution(mesh):
    line = mesh.shape["tile"] == 4 and mesh.shape["step"] == 8
    return jax.shard_map(
        local_line if line else local_general,
        mesh=mesh,
        in_specs=(
            P("step", "tile", None, None),
            P("step", "tile", None, None),
            P("step", "tile", None),
            P("step", "tile", None),
            P("tile", None),
            P("step", "tile"),
        ),
        out_specs=(P("tile", "step", None), P("tile", "step", None)),
        check_vma=False,
    )
```

```python
import functools

import jax
import jax.numpy as jnp
from jax import lax
from jax.experimental import pallas as pl
from jax.experimental.pallas import tpu as pltpu
from jax.sharding import PartitionSpec as P

HIGH = lax.Precision.HIGH


def mm(spec, *arrays):
    return jnp.einsum(spec, *arrays, precision=HIGH, preferred_element_type=jnp.float32)


def inverse_factor(gram):
    lower = jnp.linalg.cholesky(gram)
    eye = jnp.eye(gram.shape[-1], dtype=gram.dtype)
    return jax.scipy.linalg.solve_triangular(lower, eye, lower=True)


def exchange(array, axis, bit):
    return lax.ppermute(array, axis, [(i, i ^ bit) for i in range(lax.axis_size(axis))])


def take(array, index, axis):
    return lax.dynamic_index_in_dim(array, index, axis, keepdims=False)


def local_general(target_left, target_right, column_left, column_right, sketch, pattern):
    left, right = target_left[:, 0], target_right[:, 0]
    tile_rows = left.shape[1]
    probes = lax.psum(mm("kbq,bp->kqp", column_left, sketch), "tile")
    col_left = lax.all_gather(column_left, "tile", axis=1, tiled=True)
    col_right = lax.all_gather(column_right, "tile", axis=1, tiled=True)
    core = mm("kbr,kbq->krq", right, col_right) * pattern[:, 0].astype(jnp.float32)[:, None, None]
    reduced = mm("krq,kqp->krp", core, probes)
    sketched = lax.psum(mm("kbr,krp->bp", left, reduced), "step")
    inverse = inverse_factor(mm("bp,bq->pq", sketched, sketched) / tile_rows)
    row_count = tile_rows // lax.axis_size("step")
    rows = lax.dynamic_slice_in_dim(sketched, lax.axis_index("step") * row_count, row_count, 0)
    projected = mm("kbr,bp->krp", left, sketched)
    returned = mm("krq,krp->kqp", core, projected)
    partial = mm("kbq,kqp->bp", col_left, returned)
    factor = lax.psum_scatter(partial, "step", scatter_dimension=0, tiled=True) / tile_rows
    return mm("bp,qp->bq", rows, inverse)[None], mm("bp,qp->bq", factor, inverse)[None]


TN = (((0,), (0,)), ((), ()))
NN = (((1,), (0,)), ((), ()))
NT = (((1,), (1,)), ((), ()))


def split(array):
    high = array.astype(jnp.bfloat16)
    return high, (array - high.astype(jnp.float32)).astype(jnp.bfloat16)


def dot3(a, b, dims):
    a_high, a_low = split(a)
    b_high, b_low = split(b)
    axis = 1 - dims[0][1][0]
    width = b.shape[axis]
    dot = functools.partial(lax.dot_general, dimension_numbers=dims, preferred_element_type=jnp.float32)
    wide = dot(a_high, jnp.concatenate([b_high, b_low], axis))
    return wide[:, :width] + wide[:, width:] + dot(a_low, b_high)


def dot_full(a, b, dims):
    return lax.dot_general(a, b, dims, precision=lax.Precision.HIGHEST, preferred_element_type=jnp.float32)


def call(kernel, outs, args, spaces="", scratch=(), cost=0):
    kinds = {"v": pltpu.VMEM, "a": pl.ANY, "s": pltpu.SMEM}
    spaces = spaces or "v" * len(args)
    shapes = [jax.ShapeDtypeStruct(shape, jnp.float32) for shape in outs]
    return pl.pallas_call(
        kernel,
        out_shape=shapes,
        in_specs=[pl.BlockSpec(memory_space=kinds[letter]) for letter in spaces],
        out_specs=[pl.BlockSpec(memory_space=pltpu.VMEM) for _ in shapes],
        scratch_shapes=list(scratch),
        compiler_params=pltpu.CompilerParams(vmem_limit_bytes=24 << 20),
        cost_estimate=pl.CostEstimate(flops=cost, bytes_accessed=1 << 20, transcendentals=0),
    )(*args)


def load(sources, places, sems):
    copies = [pltpu.make_async_copy(source, place, sems.at[i]) for i, (source, place) in enumerate(zip(sources, places))]
    for copy in copies:
        copy.start()
    for copy in copies:
        copy.wait()


def core_kernel(planes, part, own_rows, first_hbm, second_hbm, probe_a, probe_b, core, sent, first, second, probe_in, sems):
    plane = lax.axis_index("tile")
    is_end = jnp.logical_or(plane == 0, plane == planes - 1)
    sources = [first_hbm, second_hbm, probe_a, probe_b]
    load(sources, [first, second, probe_in.at[0], probe_in.at[1]], sems)
    sent[pl.ds(2, 2)] = probe_in[0] + probe_in[1]

    @pl.when(is_end)
    def _():
        for k in range(2):
            core[k] = part[k] + dot3(own_rows[k], second[k], TN)
            sent[k] = jnp.zeros_like(sent[k])

    @pl.when(jnp.logical_not(is_end))
    def _():
        for k in range(2):
            core[k] = part[k] + dot3(own_rows[k], first[k], TN)
            sent[k] = dot3(second[k], first[k], TN)


def reduced_kernel(core, sent, got_hbm, probe_a, probe_b, pattern, both, got, probe_in, sems):
    load([got_hbm, probe_a, probe_b], [got, probe_in.at[0], probe_in.at[1]], sems)
    for k in range(2):
        c = (core[k] + got[k]) * pattern[k, 0].astype(jnp.float32)
        probe = (probe_in[0, k] + probe_in[1, k]) + (sent[2 + k] + got[2 + k])
        both[k] = dot3(c, probe, NN)
        both[2 + k] = c


def start_rows(left, left_other, held, sems, chips, rows):
    position = lax.axis_index("step")
    chip, bit = position // 2, position % 2
    copies = []
    for i in range(chips):
        block = jnp.bitwise_xor(chip, i)
        mine = left.at[:, 0, pl.ds(pl.multiple_of((block * 2 + bit) * rows, rows), rows), :]
        copies.append((
            pltpu.make_async_copy(mine, held.at[i, pl.ds(0, 2)], sems.at[2 * i]),
            pltpu.make_async_copy(left_other.at[:, block], held.at[i, pl.ds(2, 2)], sems.at[2 * i + 1]),
        ))
    for pair in copies:
        for copy in pair:
            copy.start()
    return copies


def y_kernel(left, left_other, both, both_other, *rest):
    *outs, held, sems = rest
    chips, rows = len(outs), outs[0].shape[0]
    copies = start_rows(left, left_other, held, sems, chips, rows)
    reduced = jnp.concatenate([both[0], both[1], both_other[0], both_other[1]], 0)
    for i, out in enumerate(outs):
        for copy in copies[i]:
            copy.wait()
        out[...] = dot3(jnp.concatenate([held[i, k] for k in range(4)], 1), reduced, NN)


def z_kernel(left, left_other, *rest):
    *ys, out, held, sems = rest
    chips, rows = len(ys), ys[0].shape[0]
    rank = out.shape[-1]
    copies = start_rows(left, left_other, held, sems, chips, rows)
    total = jnp.zeros((rank, 5 * rank), jnp.float32)
    dot = functools.partial(lax.dot_general, dimension_numbers=TN, preferred_element_type=jnp.float32)
    for i, y in enumerate(ys):
        y_here = y[...]
        for copy in copies[i]:
            copy.wait()
        beside = jnp.concatenate([held[i, 2], held[i, 3], held[i, 0], held[i, 1], y_here], 1)
        b_high, b_low = split(beside)
        a_high, a_low = split(y_here)
        total += dot(a_high, b_high) + dot(a_high, b_low) + dot(a_low, b_high)
    for k in range(5):
        out[k] = total[:, k * rank:(k + 1) * rank]


def w_kernel(planes, sent, got, both, both_other, own, near, inner, inner_far, outer, last, *rest):
    *outs, held, sems = rest
    plane = lax.axis_index("tile")
    chip = lax.axis_index("step") // 2
    is_end = jnp.logical_or(plane == 0, plane == planes - 1)

    def pick(i, wanted, source):
        @pl.when(wanted)
        def _():
            pltpu.make_async_copy(source, held.at[i], sems.at[i]).start()

    for i in range(planes):
        block = jnp.bitwise_xor(chip, i)
        apart = jnp.bitwise_xor(block, plane)
        pick(i, apart == 0, own)
        pick(i, apart == 1, near)
        pick(i, jnp.logical_and(apart == 2, is_end), outer)
        pick(i, jnp.logical_and(apart == 2, jnp.logical_not(is_end)), inner_far)
        pick(i, jnp.logical_and(apart == 3, is_end), last)
        pick(i, jnp.logical_and(apart == 3, jnp.logical_not(is_end)), inner)
    returned = []
    for k in range(2):
        returned.append(dot3(sent[2 + k] + got[k], both[2 + k], NN))
    for k in range(2):
        returned.append(dot3(sent[k] + got[2 + k], both_other[2 + k], NN))
    returned = jnp.concatenate(returned, 1)
    for i, out in enumerate(outs):
        pltpu.make_async_copy(own, held.at[i], sems.at[i]).wait()
        out[...] = dot3(jnp.concatenate([held[i, k] for k in range(4)], 1), returned, NT)


def basis_kernel(tile_rows, width, sent, got, y_rows, basis, inverse):
    rank = inverse.shape[0]
    scaled = (sent[4] + got[4]) * (1.0 / tile_rows)
    eye = (lax.broadcasted_iota(jnp.int32, (rank, rank), 0) == lax.broadcasted_iota(jnp.int32, (rank, rank), 1))
    work = jnp.concatenate([scaled, eye.astype(jnp.float32)], 1)
    done = []
    for begin in range(0, rank, width):
        panel = work[:width]
        row_index = lax.broadcasted_iota(jnp.int32, (width, 1), 0)
        scale = jnp.zeros((width, 1), jnp.float32)
        for j in range(width):
            column = panel[:, begin + j:begin + j + 1]
            pivot = panel[j:j + 1, begin + j:begin + j + 1]
            factor = jnp.where(row_index > j, column * (1.0 / pivot), 0.0)
            scale = jnp.where(row_index == j, lax.rsqrt(pivot), scale)
            panel = panel - factor * panel[j:j + 1]
        panel = panel * scale
        done.append(panel[:, rank:])
        if begin + width < rank:
            work = work[width:] - dot_full(panel[:, begin + width:rank], panel, TN)
    lower_inverse = jnp.concatenate(done, 0)
    inverse[...] = lower_inverse
    basis[...] = dot_full(y_rows[...], lower_inverse, NT)


def factor_kernel(tile_rows, a, b, c, d, inverse, factor):
    total = (a[...] + b[...] + c[...] + d[...]) * (1.0 / tile_rows)
    factor[...] = dot_full(total, inverse[...], NT)


def local_line(target_left, target_right, column_left, column_right, sketch, pattern):
    tile_rows, rank = target_left.shape[2:]
    planes = lax.axis_size("tile")
    chips = lax.axis_size("step") // 2
    plane = lax.axis_index("tile")
    core_bit = lax.axis_index("step") % 2
    chip = lax.axis_index("step") // 2
    row_count = tile_rows // (2 * chips)
    is_end = jnp.logical_or(plane == 0, plane == planes - 1)
    outer_pairs, inner_pairs = [(0, 1), (1, 0), (2, 3), (3, 2)], [(1, 2), (2, 1)]
    outward = [(1, 0), (2, 3)]

    def across(array, pairs):
        return lax.ppermute(array, "tile", pairs)

    near = across(column_right, outer_pairs)
    inner = across(column_right, inner_pairs)
    probes = mm("kbq,bp->kqp", column_left, sketch)
    probes_near = across(probes, outer_pairs)
    probes_inner = across(probes, inner_pairs)
    right_blocks = target_right.reshape(2, planes, -1, rank)

    def block(index):
        return take(right_blocks, index, 1)

    left_split = target_left.reshape(2, chips, 2, row_count, rank)
    left_other = exchange(take(left_split, 1 - core_bit, 2), "step", 1)
    col_split = column_left.reshape(2, 2, row_count, rank)
    col_half = jnp.concatenate([take(col_split, core_bit, 1), exchange(take(col_split, 1 - core_bit, 1), "step", 1)])

    lent_rows = block(planes - 1 - plane)
    inner_far = across(near, inner_pairs)
    outer = across(jnp.where(is_end, lent_rows, inner), outer_pairs)
    part = (
        mm("kbr,kbq->krq", block(plane), column_right)
        + mm("kbr,kbq->krq", block(plane ^ 1), near)
        + mm("kbr,kbq->krq", block(jnp.where(is_end, plane, planes - 1 - plane)), inner)
    )
    part, probes_near, col_half = lax.optimization_barrier((part, probes_near, col_half))
    probes_far = across(probes_near, inner_pairs)
    col_inner = across(col_half, inner_pairs)
    far_rows = block(plane ^ 2)
    rows_per_plane = column_right.shape[1]
    core, lent = call(
        functools.partial(core_kernel, planes),
        [(2, rank, rank), (4, rank, rank)],
        [part, far_rows, inner_far, outer, probes_inner, probes_far],
        "vvaaaa",
        [pltpu.VMEM((2, rows_per_plane, rank), jnp.float32)] * 2
        + [pltpu.VMEM((2, 2, rank, rank), jnp.float32), pltpu.SemaphoreType.DMA((4,))],
    )
    lent_got = across(lent, outward)
    col_half, _ = lax.optimization_barrier((col_half, lent))
    col_near = across(col_half, outer_pairs)

    reduced_scratch = [pltpu.VMEM((4, rank, rank), jnp.float32), pltpu.VMEM((2, 2, rank, rank), jnp.float32)]
    reduced_scratch += [pltpu.SemaphoreType.DMA((3,))]
    (both,) = call(reduced_kernel, [(4, rank, rank)], [core, lent, lent_got, probes, probes_near, pattern], "vvaaas", reduced_scratch)
    both_other = exchange(both, "step", 1)
    rows_scratch = [pltpu.VMEM((chips, 4, row_count, rank), jnp.float32), pltpu.SemaphoreType.DMA((2 * chips,))]
    y_parts = call(y_kernel, [(row_count, rank)] * chips, [target_left, left_other, both, both_other], "aavv", rows_scratch)
    y_got = [exchange(y_parts[bit], "step", 2 * bit) for bit in range(1, chips)]
    y_got[0], col_near_held, col_inner_held = lax.optimization_barrier((y_got[0], col_near, col_inner))
    col_inner_far = across(col_near_held, inner_pairs)
    col_outer = across(col_inner_held, outward)
    y_rows = y_parts[0]
    for got in y_got:
        y_rows = y_rows + got
    y_all = [y_rows] + [exchange(y_rows, "step", 2 * bit) for bit in range(1, chips)]
    y_all[1], col_inner_far_held = lax.optimization_barrier((y_all[1], col_inner_far))
    col_last = across(col_inner_far_held, outward)
    (sent,) = call(z_kernel, [(5, rank, rank)], [target_left, left_other, *y_all], "aa" + "v" * chips, rows_scratch)
    got = exchange(sent, "step", 1)
    w_parts = call(
        functools.partial(w_kernel, planes),
        [(row_count, rank)] * planes,
        [sent, got, both, both_other, col_half, col_near, col_inner, col_inner_far, col_outer, col_last],
        "vvvvaaaaaa",
        [pltpu.VMEM((planes, 4, row_count, rank), jnp.float32), pltpu.SemaphoreType.DMA((planes,))],
    )
    w_got = [exchange(w_parts[bit], "step", 2 * bit) for bit in range(1, chips)]
    basis, inverse = call(
        functools.partial(basis_kernel, tile_rows, 32), [(row_count, rank), (rank, rank)], [sent, got, y_rows], cost=10**9
    )
    (factor,) = call(functools.partial(factor_kernel, tile_rows), [(row_count, rank)], [w_parts[0], *w_got, inverse])
    return basis[None], factor[None]


def solution(mesh):
    line = mesh.shape["tile"] == 4 and mesh.shape["step"] == 8
    return jax.shard_map(
        local_line if line else local_general,
        mesh=mesh,
        in_specs=(
            P("step", "tile", None, None),
            P("step", "tile", None, None),
            P("step", "tile", None),
            P("step", "tile", None),
            P("tile", None),
            P("step", "tile"),
        ),
        out_specs=(P("tile", "step", None), P("tile", "step", None)),
        check_vma=False,
    )
```

```python
import functools

import jax
import jax.numpy as jnp
from jax import lax
from jax.experimental import pallas as pl
from jax.experimental.pallas import tpu as pltpu
from jax.sharding import PartitionSpec as P

HIGH = lax.Precision.HIGH


def mm(spec, *arrays):
    return jnp.einsum(spec, *arrays, precision=HIGH, preferred_element_type=jnp.float32)


def inverse_factor(gram):
    lower = jnp.linalg.cholesky(gram)
    eye = jnp.eye(gram.shape[-1], dtype=gram.dtype)
    return jax.scipy.linalg.solve_triangular(lower, eye, lower=True)


def exchange(array, axis, bit):
    return lax.ppermute(array, axis, [(i, i ^ bit) for i in range(lax.axis_size(axis))])


def take(array, index, axis):
    return lax.dynamic_index_in_dim(array, index, axis, keepdims=False)


def local_general(target_left, target_right, column_left, column_right, sketch, pattern):
    left, right = target_left[:, 0], target_right[:, 0]
    tile_rows = left.shape[1]
    probes = lax.psum(mm("kbq,bp->kqp", column_left, sketch), "tile")
    col_left = lax.all_gather(column_left, "tile", axis=1, tiled=True)
    col_right = lax.all_gather(column_right, "tile", axis=1, tiled=True)
    core = mm("kbr,kbq->krq", right, col_right) * pattern[:, 0].astype(jnp.float32)[:, None, None]
    reduced = mm("krq,kqp->krp", core, probes)
    sketched = lax.psum(mm("kbr,krp->bp", left, reduced), "step")
    inverse = inverse_factor(mm("bp,bq->pq", sketched, sketched) / tile_rows)
    row_count = tile_rows // lax.axis_size("step")
    rows = lax.dynamic_slice_in_dim(sketched, lax.axis_index("step") * row_count, row_count, 0)
    projected = mm("kbr,bp->krp", left, sketched)
    returned = mm("krq,krp->kqp", core, projected)
    partial = mm("kbq,kqp->bp", col_left, returned)
    factor = lax.psum_scatter(partial, "step", scatter_dimension=0, tiled=True) / tile_rows
    return mm("bp,qp->bq", rows, inverse)[None], mm("bp,qp->bq", factor, inverse)[None]


TN = (((0,), (0,)), ((), ()))
NN = (((1,), (0,)), ((), ()))
NT = (((1,), (1,)), ((), ()))


def split(array):
    high = array.astype(jnp.bfloat16)
    return high, (array - high.astype(jnp.float32)).astype(jnp.bfloat16)


def dot3(a, b, dims):
    a_high, a_low = split(a)
    b_high, b_low = split(b)
    axis = 1 - dims[0][1][0]
    width = b.shape[axis]
    dot = functools.partial(lax.dot_general, dimension_numbers=dims, preferred_element_type=jnp.float32)
    wide = dot(a_high, jnp.concatenate([b_high, b_low], axis))
    return wide[:, :width] + wide[:, width:] + dot(a_low, b_high)


def dot_full(a, b, dims):
    return lax.dot_general(a, b, dims, precision=lax.Precision.HIGHEST, preferred_element_type=jnp.float32)


def call(kernel, outs, args, spaces="", scratch=(), cost=0, limit=24, stored=()):
    kinds = {"v": pltpu.VMEM, "a": pl.ANY, "l": pltpu.HBM, "h": pltpu.HBM, "s": pltpu.SMEM}
    spaces = spaces or "l" * len(args)
    loaded = [i for i, letter in enumerate(spaces) if letter == "l"]
    shapes = [jax.ShapeDtypeStruct(shape, jnp.float32) for shape in outs]
    held = [pltpu.VMEM(args[i].shape, jnp.float32) for i in loaded] + [pltpu.VMEM(outs[i], jnp.float32) for i in stored]
    held.append(pltpu.SemaphoreType.DMA((len(held) + 1,)))

    def body(*refs):
        own, sems = refs[-len(held):-1], refs[-1]
        refs = list(refs[:-len(held)])
        copies = []
        for n, i in enumerate(loaded):
            copies.append(pltpu.make_async_copy(refs[i], own[n], sems.at[n]))
            copies[-1].start()
            refs[i] = own[n]
        after = []
        for n, i in enumerate(stored, len(loaded)):
            after.append(pltpu.make_async_copy(own[n], refs[len(args) + i], sems.at[n]))
            refs[len(args) + i] = own[n]
        for copy in copies:
            copy.wait()
        kernel(*refs)
        for copy in after:
            copy.start()
        for copy in after:
            copy.wait()

    return pl.pallas_call(
        body,
        out_shape=shapes,
        in_specs=[pl.BlockSpec(memory_space=kinds[letter]) for letter in spaces],
        out_specs=[pl.BlockSpec(memory_space=pltpu.HBM if i in stored else pltpu.VMEM) for i in range(len(outs))],
        scratch_shapes=list(scratch) + held,
        compiler_params=pltpu.CompilerParams(vmem_limit_bytes=limit << 20),
        cost_estimate=pl.CostEstimate(flops=cost, bytes_accessed=0, transcendentals=0),
    )(*args)


def load(sources, places, sems):
    copies = [pltpu.make_async_copy(source, place, sems.at[i]) for i, (source, place) in enumerate(zip(sources, places))]
    for copy in copies:
        copy.start()
    for copy in copies:
        copy.wait()


def pack_kernel(column_right, column_left, sketch, message, sem):
    rows = column_right.shape[1]
    copy = pltpu.make_async_copy(column_right, message.at[:, pl.ds(0, rows)], sem)
    copy.start()
    for k in range(message.shape[0]):
        message[k, pl.ds(rows, column_left.shape[2])] = dot3(column_left[k], sketch[...], TN)
    copy.wait()


def core_kernel(planes, part, own_rows, own_hbm, near_hbm, inner_hbm, first_hbm, second_hbm, core, sent, probe, *held):
    first, second, probe_in, sems = held
    plane = lax.axis_index("tile")
    is_end = jnp.logical_or(plane == 0, plane == planes - 1)
    rows, rank = own_rows.shape[1:]
    terms = [ref.at[:, pl.ds(rows, rank)] for ref in (own_hbm, near_hbm, inner_hbm)]
    load([first_hbm, second_hbm, *terms], [first, second, *(probe_in.at[i] for i in range(3))], sems)
    probe[...] = probe_in[0] + probe_in[1]
    sent[pl.ds(2, 2)] = probe_in[2] + first[:, rows:]

    @pl.when(is_end)
    def _():
        for k in range(2):
            core[k] = part[k] + dot3(own_rows[k], second[k], TN)
            sent[k] = jnp.zeros_like(sent[k])

    @pl.when(jnp.logical_not(is_end))
    def _():
        for k in range(2):
            core[k] = part[k] + dot3(own_rows[k], first[k, :rows], TN)
            sent[k] = dot3(second[k], first[k, :rows], TN)


def reduced_kernel(core, sent, got, probe, pattern, both):
    for k in range(2):
        c = (core[k] + got[k]) * pattern[k, 0].astype(jnp.float32)
        both[k] = dot3(c, probe[k] + (sent[2 + k] + got[2 + k]), NN)
        both[2 + k] = c


def start_rows(left, left_other, held, sems, chips, rows):
    position = lax.axis_index("step")
    chip, bit = position // 2, position % 2
    copies = []
    for i in range(chips):
        block = jnp.bitwise_xor(chip, i)
        mine = left.at[:, 0, pl.ds(pl.multiple_of((block * 2 + bit) * rows, rows), rows), :]
        copies.append((
            pltpu.make_async_copy(mine, held.at[i, pl.ds(0, 2)], sems.at[2 * i]),
            pltpu.make_async_copy(left_other.at[:, block], held.at[i, pl.ds(2, 2)], sems.at[2 * i + 1]),
        ))
    for pair in copies:
        for copy in pair:
            copy.start()
    return copies


def y_kernel(left, left_other, both, both_other, *rest):
    *outs, held, sems = rest
    chips, rows = len(outs), outs[0].shape[0]
    copies = start_rows(left, left_other, held, sems, chips, rows)
    reduced = jnp.concatenate([both[0], both[1], both_other[0], both_other[1]], 0)
    for i, out in enumerate(outs):
        for copy in copies[i]:
            copy.wait()
        out[...] = dot3(jnp.concatenate([held[i, k] for k in range(4)], 1), reduced, NN)


def z_kernel(left, left_other, *rest):
    *ys, out, held, sems = rest
    chips, rows = len(ys), ys[0].shape[0]
    rank = out.shape[-1]
    copies = start_rows(left, left_other, held, sems, chips, rows)
    total = jnp.zeros((rank, 5 * rank), jnp.float32)
    dot = functools.partial(lax.dot_general, dimension_numbers=TN, preferred_element_type=jnp.float32)
    for i, y in enumerate(ys):
        y_here = y[...]
        for copy in copies[i]:
            copy.wait()
        beside = jnp.concatenate([held[i, 2], held[i, 3], held[i, 0], held[i, 1], y_here], 1)
        b_high, b_low = split(beside)
        a_high, a_low = split(y_here)
        total += dot(a_high, b_high) + dot(a_high, b_low) + dot(a_low, b_high)
    for k in range(5):
        out[k] = total[:, k * rank:(k + 1) * rank]


def w_kernel(planes, sent, got, both, both_other, own, near, inner, inner_far, outer, last, *rest):
    *outs, held, sems = rest
    plane = lax.axis_index("tile")
    chip = lax.axis_index("step") // 2
    is_end = jnp.logical_or(plane == 0, plane == planes - 1)

    def pick(i, wanted, source):
        @pl.when(wanted)
        def _():
            pltpu.make_async_copy(source, held.at[i], sems.at[i]).start()

    for i in range(planes):
        block = jnp.bitwise_xor(chip, i)
        apart = jnp.bitwise_xor(block, plane)
        pick(i, apart == 0, own)
        pick(i, apart == 1, near)
        pick(i, jnp.logical_and(apart == 2, is_end), outer)
        pick(i, jnp.logical_and(apart == 2, jnp.logical_not(is_end)), inner_far)
        pick(i, jnp.logical_and(apart == 3, is_end), last)
        pick(i, jnp.logical_and(apart == 3, jnp.logical_not(is_end)), inner)
    returned = []
    for k in range(2):
        returned.append(dot3(sent[2 + k] + got[k], both[2 + k], NN))
    for k in range(2):
        returned.append(dot3(sent[k] + got[2 + k], both_other[2 + k], NN))
    returned = jnp.concatenate(returned, 1)
    for i, out in enumerate(outs):
        pltpu.make_async_copy(own, held.at[i], sems.at[i]).wait()
        out[...] = dot3(jnp.concatenate([held[i, k] for k in range(4)], 1), returned, NT)


def basis_kernel(tile_rows, width, sent, got, y_rows, basis, inverse):
    rank = inverse.shape[0]
    scaled = (sent[4] + got[4]) * (1.0 / tile_rows)
    eye = (lax.broadcasted_iota(jnp.int32, (rank, rank), 0) == lax.broadcasted_iota(jnp.int32, (rank, rank), 1))
    work = jnp.concatenate([scaled, eye.astype(jnp.float32)], 1)
    done = []
    for begin in range(0, rank, width):
        panel = work[:width]
        row_index = lax.broadcasted_iota(jnp.int32, (width, 1), 0)
        scale = jnp.zeros((width, 1), jnp.float32)
        for j in range(width):
            column = panel[:, begin + j:begin + j + 1]
            pivot = panel[j:j + 1, begin + j:begin + j + 1]
            factor = jnp.where(row_index > j, column * (1.0 / pivot), 0.0)
            scale = jnp.where(row_index == j, lax.rsqrt(pivot), scale)
            panel = panel - factor * panel[j:j + 1]
        panel = panel * scale
        done.append(panel[:, rank:])
        if begin + width < rank:
            work = work[width:] - dot_full(panel[:, begin + width:rank], panel, TN)
    lower_inverse = jnp.concatenate(done, 0)
    inverse[...] = lower_inverse
    basis[...] = dot_full(y_rows[...], lower_inverse, NT)


def factor_kernel(tile_rows, a, b, c, d, inverse, factor):
    total = (a[...] + b[...] + c[...] + d[...]) * (1.0 / tile_rows)
    factor[...] = dot_full(total, inverse[...], NT)


def local_line(target_left, target_right, column_left, column_right, sketch, pattern):
    tile_rows, rank = target_left.shape[2:]
    planes = lax.axis_size("tile")
    chips = lax.axis_size("step") // 2
    plane = lax.axis_index("tile")
    core_bit = lax.axis_index("step") % 2
    chip = lax.axis_index("step") // 2
    row_count = tile_rows // (2 * chips)
    is_end = jnp.logical_or(plane == 0, plane == planes - 1)
    outer_pairs, inner_pairs = [(0, 1), (1, 0), (2, 3), (3, 2)], [(1, 2), (2, 1)]
    outward = [(1, 0), (2, 3)]

    def across(array, pairs):
        return lax.ppermute(array, "tile", pairs)

    rows = column_right.shape[1]
    (message,) = call(
        pack_kernel, [(2, rows + rank, rank)], [column_right, column_left, sketch], "hll", [pltpu.SemaphoreType.DMA], limit=60
    )
    near = across(message, outer_pairs)
    inner = across(message, inner_pairs)
    right_blocks = target_right.reshape(2, planes, -1, rank)

    def block(index):
        return take(right_blocks, index, 1)

    left_split = target_left.reshape(2, chips, 2, row_count, rank)
    left_other = exchange(take(left_split, 1 - core_bit, 2), "step", 1)
    col_split = column_left.reshape(2, 2, row_count, rank)
    col_half = jnp.concatenate([take(col_split, core_bit, 1), exchange(take(col_split, 1 - core_bit, 1), "step", 1)])

    lent_rows = block(planes - 1 - plane)
    inner_far = across(near, inner_pairs)
    outer = across(jnp.where(is_end, lent_rows, inner[:, :rows]), outer_pairs)
    part = (
        mm("kbr,kbq->krq", block(plane), column_right)
        + mm("kbr,kbq->krq", block(plane ^ 1), near[:, :rows])
        + mm("kbr,kbq->krq", block(jnp.where(is_end, plane, planes - 1 - plane)), inner[:, :rows])
    )
    part, col_half = lax.optimization_barrier((part, col_half))
    col_inner = across(col_half, inner_pairs)
    col_near = across(col_half, outer_pairs)
    core, lent, probe = call(
        functools.partial(core_kernel, planes),
        [(2, rank, rank), (4, rank, rank), (2, rank, rank)],
        [part, block(plane ^ 2), message, near, inner, inner_far, outer],
        "vvhhhhh",
        [pltpu.VMEM((2, rows + rank, rank), jnp.float32), pltpu.VMEM((2, rows, rank), jnp.float32)]
        + [pltpu.VMEM((3, 2, rank, rank), jnp.float32), pltpu.SemaphoreType.DMA((5,))],
        stored=(0, 1, 2),
        limit=60,
    )
    lent_got = across(lent, outer_pairs)
    _, col_near_held, col_inner_held = lax.optimization_barrier((lent_got, col_near, col_inner))
    col_inner_far = across(col_near_held, inner_pairs)
    col_outer = across(col_inner_held, outward)
    col_outer, col_inner_far = lax.optimization_barrier((col_outer, col_inner_far))
    (both,) = call(reduced_kernel, [(4, rank, rank)], [core, lent, lent_got, probe, pattern], "lllls", limit=60)
    both_other = exchange(both, "step", 1)
    rows_scratch = [pltpu.VMEM((chips, 4, row_count, rank), jnp.float32), pltpu.SemaphoreType.DMA((2 * chips,))]
    y_parts = call(y_kernel, [(row_count, rank)] * chips, [target_left, left_other, both, both_other], "aavv", rows_scratch)
    y_rows = y_parts[0]
    for bit in range(1, chips):
        y_rows = y_rows + exchange(y_parts[bit], "step", 2 * bit)
    y_all = [y_rows] + [exchange(y_rows, "step", 2 * bit) for bit in range(1, chips)]
    _, col_last = lax.optimization_barrier((y_rows, col_inner_far))
    col_last = across(col_last, outward)
    (sent,) = call(z_kernel, [(5, rank, rank)], [target_left, left_other, *y_all], "aa" + "v" * chips, rows_scratch)
    got = exchange(sent, "step", 1)
    w_parts = call(
        functools.partial(w_kernel, planes),
        [(row_count, rank)] * planes,
        [sent, got, both, both_other, col_half, col_near, col_inner, col_inner_far, col_outer, col_last],
        "vvvvhhhhhh",
        [pltpu.VMEM((planes, 4, row_count, rank), jnp.float32), pltpu.SemaphoreType.DMA((planes,))],
    )
    w_got = [exchange(w_parts[bit], "step", 2 * bit) for bit in range(1, chips)]
    basis, inverse = call(
        functools.partial(basis_kernel, tile_rows, 32), [(row_count, rank), (rank, rank)], [sent, got, y_rows], "vvv", cost=10**9
    )
    (factor,) = call(functools.partial(factor_kernel, tile_rows), [(row_count, rank)], [w_parts[0], *w_got, inverse], "v" * (chips + 1))
    return basis[None], factor[None]


def solution(mesh):
    line = mesh.shape["tile"] == 4 and mesh.shape["step"] == 8
    return jax.shard_map(
        local_line if line else local_general,
        mesh=mesh,
        in_specs=(
            P("step", "tile", None, None),
            P("step", "tile", None, None),
            P("step", "tile", None),
            P("step", "tile", None),
            P("tile", None),
            P("step", "tile"),
        ),
        out_specs=(P("tile", "step", None), P("tile", "step", None)),
        check_vma=False,
    )
```

```python
import functools

import jax
import jax.numpy as jnp
from jax import lax
from jax.experimental import pallas as pl
from jax.experimental.pallas import tpu as pltpu
from jax.sharding import PartitionSpec as P

HIGH = lax.Precision.HIGH


def mm(spec, *arrays):
    return jnp.einsum(spec, *arrays, precision=HIGH, preferred_element_type=jnp.float32)


def inverse_factor(gram):
    lower = jnp.linalg.cholesky(gram)
    eye = jnp.eye(gram.shape[-1], dtype=gram.dtype)
    return jax.scipy.linalg.solve_triangular(lower, eye, lower=True)


def exchange(array, axis, bit):
    return lax.ppermute(array, axis, [(i, i ^ bit) for i in range(lax.axis_size(axis))])


def take(array, index, axis):
    return lax.dynamic_index_in_dim(array, index, axis, keepdims=False)


def local_general(target_left, target_right, column_left, column_right, sketch, pattern):
    left, right = target_left[:, 0], target_right[:, 0]
    tile_rows = left.shape[1]
    probes = lax.psum(mm("kbq,bp->kqp", column_left, sketch), "tile")
    col_left = lax.all_gather(column_left, "tile", axis=1, tiled=True)
    col_right = lax.all_gather(column_right, "tile", axis=1, tiled=True)
    core = mm("kbr,kbq->krq", right, col_right) * pattern[:, 0].astype(jnp.float32)[:, None, None]
    reduced = mm("krq,kqp->krp", core, probes)
    sketched = lax.psum(mm("kbr,krp->bp", left, reduced), "step")
    inverse = inverse_factor(mm("bp,bq->pq", sketched, sketched) / tile_rows)
    row_count = tile_rows // lax.axis_size("step")
    rows = lax.dynamic_slice_in_dim(sketched, lax.axis_index("step") * row_count, row_count, 0)
    projected = mm("kbr,bp->krp", left, sketched)
    returned = mm("krq,krp->kqp", core, projected)
    partial = mm("kbq,kqp->bp", col_left, returned)
    factor = lax.psum_scatter(partial, "step", scatter_dimension=0, tiled=True) / tile_rows
    return mm("bp,qp->bq", rows, inverse)[None], mm("bp,qp->bq", factor, inverse)[None]


TN = (((0,), (0,)), ((), ()))
NN = (((1,), (0,)), ((), ()))
NT = (((1,), (1,)), ((), ()))


def split(array):
    high = array.astype(jnp.bfloat16)
    return high, (array - high.astype(jnp.float32)).astype(jnp.bfloat16)


def dot3(a, b, dims):
    a_high, a_low = split(a)
    b_high, b_low = split(b)
    axis = 1 - dims[0][1][0]
    width = b.shape[axis]
    dot = functools.partial(lax.dot_general, dimension_numbers=dims, preferred_element_type=jnp.float32)
    wide = dot(a_high, jnp.concatenate([b_high, b_low], axis))
    return wide[:, :width] + wide[:, width:] + dot(a_low, b_high)


def dot_full(a, b, dims):
    return lax.dot_general(a, b, dims, precision=lax.Precision.HIGHEST, preferred_element_type=jnp.float32)


def call(kernel, outs, args, spaces="", scratch=(), cost=0):
    kinds = {"v": pltpu.VMEM, "a": pl.ANY, "s": pltpu.SMEM}
    spaces = spaces or "v" * len(args)
    shapes = [jax.ShapeDtypeStruct(shape, jnp.float32) for shape in outs]
    return pl.pallas_call(
        kernel,
        out_shape=shapes,
        in_specs=[pl.BlockSpec(memory_space=kinds[letter]) for letter in spaces],
        out_specs=[pl.BlockSpec(memory_space=pltpu.VMEM) for _ in shapes],
        scratch_shapes=list(scratch),
        compiler_params=pltpu.CompilerParams(vmem_limit_bytes=24 << 20),
        cost_estimate=pl.CostEstimate(flops=cost, bytes_accessed=0, transcendentals=0),
    )(*args)


def core_kernel(planes, part, own_rows, first, second, probe_far, core, lent):
    lent[pl.ds(2, 2)] = probe_far[...]
    plane = lax.axis_index("tile")
    is_end = jnp.logical_or(plane == 0, plane == planes - 1)

    @pl.when(is_end)
    def _():
        for k in range(2):
            core[k] = part[k] + dot3(own_rows[k], second[k], TN)
            lent[k] = jnp.zeros_like(core[k])

    @pl.when(jnp.logical_not(is_end))
    def _():
        for k in range(2):
            core[k] = part[k] + dot3(own_rows[k], first[k], TN)
            lent[k] = dot3(second[k], first[k], TN)


def reduced_kernel(core, lent, probe_here, probe_far, pattern, both):
    for k in range(2):
        weight = pattern[k, 0].astype(jnp.float32)
        c = (core[k] + lent[k]) * weight
        both[k] = dot3(c, probe_here[k] + probe_far[k] + lent[2 + k], NN)
        both[2 + k] = c


def start_rows(left, left_other, held, sems, chips, rows):
    position = lax.axis_index("step")
    chip, bit = position // 2, position % 2
    copies = []
    for i in range(chips):
        block = jnp.bitwise_xor(chip, i)
        mine = left.at[:, 0, pl.ds(pl.multiple_of((block * 2 + bit) * rows, rows), rows), :]
        copies.append((
            pltpu.make_async_copy(mine, held.at[i, pl.ds(0, 2)], sems.at[2 * i]),
            pltpu.make_async_copy(left_other.at[:, block], held.at[i, pl.ds(2, 2)], sems.at[2 * i + 1]),
        ))
    for pair in copies:
        for copy in pair:
            copy.start()
    return copies


def y_kernel(left, left_other, both, both_other, *rest):
    *outs, held, sems = rest
    chips, rows = len(outs), outs[0].shape[0]
    copies = start_rows(left, left_other, held, sems, chips, rows)
    reduced = jnp.concatenate([both[0], both[1], both_other[0], both_other[1]], 0)
    for i, out in enumerate(outs):
        for copy in copies[i]:
            copy.wait()
        out[...] = dot3(jnp.concatenate([held[i, k] for k in range(4)], 1), reduced, NN)


def z_kernel(left, left_other, *rest):
    *ys, out, held, sems = rest
    chips, rows = len(ys), ys[0].shape[0]
    rank = out.shape[-1]
    copies = start_rows(left, left_other, held, sems, chips, rows)
    total = jnp.zeros((rank, 5 * rank), jnp.float32)
    dot = functools.partial(lax.dot_general, dimension_numbers=TN, preferred_element_type=jnp.float32)
    for i, y in enumerate(ys):
        y_here = y[...]
        for copy in copies[i]:
            copy.wait()
        beside = jnp.concatenate([held[i, 2], held[i, 3], held[i, 0], held[i, 1], y_here], 1)
        b_high, b_low = split(beside)
        a_high, a_low = split(y_here)
        total += dot(a_high, b_high) + dot(a_high, b_low) + dot(a_low, b_high)
    for k in range(5):
        out[k] = total[:, k * rank:(k + 1) * rank]


def w_kernel(planes, sent, got, both, both_other, own, near, inner, inner_far, outer, last, *rest):
    *outs, held, sems = rest
    plane = lax.axis_index("tile")
    chip = lax.axis_index("step") // 2
    is_end = jnp.logical_or(plane == 0, plane == planes - 1)

    def pick(i, wanted, source):
        @pl.when(wanted)
        def _():
            pltpu.make_async_copy(source, held.at[i], sems.at[i]).start()

    for i in range(planes):
        block = jnp.bitwise_xor(chip, i)
        apart = jnp.bitwise_xor(block, plane)
        pick(i, apart == 0, own)
        pick(i, apart == 1, near)
        pick(i, jnp.logical_and(apart == 2, is_end), outer)
        pick(i, jnp.logical_and(apart == 2, jnp.logical_not(is_end)), inner_far)
        pick(i, jnp.logical_and(apart == 3, is_end), last)
        pick(i, jnp.logical_and(apart == 3, jnp.logical_not(is_end)), inner)
    returned = []
    for k in range(2):
        returned.append(dot3(sent[2 + k] + got[k], both[2 + k], NN))
    for k in range(2):
        returned.append(dot3(sent[k] + got[2 + k], both_other[2 + k], NN))
    returned = jnp.concatenate(returned, 1)
    for i, out in enumerate(outs):
        pltpu.make_async_copy(own, held.at[i], sems.at[i]).wait()
        out[...] = dot3(jnp.concatenate([held[i, k] for k in range(4)], 1), returned, NT)


def basis_kernel(tile_rows, width, group, sent, got, y_rows, basis, inverse):
    rank = inverse.shape[0]
    left = (sent[4] + got[4]) * (1.0 / tile_rows)
    index = lax.broadcasted_iota(jnp.int32, (rank, rank), 0)
    right = (index == lax.broadcasted_iota(jnp.int32, (rank, rank), 1)).astype(jnp.float32)
    row_index = lax.broadcasted_iota(jnp.int32, (width, rank), 0)
    done = []
    for begin in range(0, rank, width):
        l, r = left[:width], right[:width]
        scale = jnp.zeros((width, rank), jnp.float32)
        for first in range(0, width, group):
            place = begin + first
            columns = [jnp.broadcast_to(l[:, place + c:place + c + 1], (width, rank)) for c in range(group)]
            for c in range(group):
                j = first + c
                pivot = columns[c][j:j + 1]
                scale = jnp.where(row_index == j, lax.rsqrt(pivot), scale)
                factor = jnp.where(row_index > j, columns[c] * (1.0 / pivot), 0.0)
                for d in range(c + 1, group):
                    columns[d] = columns[d] - factor * columns[d][j:j + 1]
                l, r = l - factor * l[j:j + 1], r - factor * r[j:j + 1]
        l, r = l * scale, r * scale
        done.append(r)
        if begin + width < rank:
            both = dot_full(l[:, begin + width:], jnp.concatenate([l, r], 1), TN)
            left, right = left[width:] - both[:, :rank], right[width:] - both[:, rank:]
    lower_inverse = jnp.concatenate(done, 0)
    inverse[...] = lower_inverse
    basis[...] = dot_full(y_rows[...], lower_inverse, NT)


def factor_kernel(tile_rows, a, b, c, d, inverse, factor):
    total = (a[...] + b[...] + c[...] + d[...]) * (1.0 / tile_rows)
    factor[...] = dot_full(total, inverse[...], NT)


def local_line(target_left, target_right, column_left, column_right, sketch, pattern):
    tile_rows, rank = target_left.shape[2:]
    planes = lax.axis_size("tile")
    chips = lax.axis_size("step") // 2
    plane = lax.axis_index("tile")
    core_bit = lax.axis_index("step") % 2
    chip = lax.axis_index("step") // 2
    row_count = tile_rows // (2 * chips)
    is_end = jnp.logical_or(plane == 0, plane == planes - 1)
    outer_pairs, inner_pairs = [(0, 1), (1, 0), (2, 3), (3, 2)], [(1, 2), (2, 1)]
    outward = [(1, 0), (2, 3)]

    def across(array, pairs):
        return lax.ppermute(array, "tile", pairs)

    near = across(column_right, outer_pairs)
    inner = across(column_right, inner_pairs)
    probes = mm("kbq,bp->kqp", column_left, sketch)
    probes = probes + across(probes, outer_pairs)
    right_blocks = target_right.reshape(2, planes, -1, rank)

    def block(index):
        return take(right_blocks, index, 1)

    inner_far = across(near, inner_pairs)
    outer = across(jnp.where(is_end, block(planes - 1 - plane), inner), outer_pairs)
    part = (
        mm("kbr,kbq->krq", block(plane), column_right)
        + mm("kbr,kbq->krq", block(plane ^ 1), near)
        + mm("kbr,kbq->krq", block(jnp.where(is_end, plane, planes - 1 - plane)), inner)
    )
    _, probes_held = lax.optimization_barrier((near, probes))
    probes_far = across(probes_held, inner_pairs)
    far_rows = block(plane ^ 2)
    core, lent = call(functools.partial(core_kernel, planes), [(2, rank, rank), (4, rank, rank)], [part, far_rows, inner_far, outer, probes_far])
    lent = across(lent, outward)

    left_split = target_left.reshape(2, chips, 2, row_count, rank)
    left_other = exchange(take(left_split, 1 - core_bit, 2), "step", 1)
    col_split = column_left.reshape(2, 2, row_count, rank)
    col_half = jnp.concatenate([take(col_split, core_bit, 1), exchange(take(col_split, 1 - core_bit, 1), "step", 1)])
    _, col_held = lax.optimization_barrier((near, col_half))
    col_near = across(col_held, outer_pairs)
    col_inner = across(col_held, inner_pairs)
    col_near, col_inner = lax.optimization_barrier((col_near, col_inner))
    col_inner_far = across(col_near, inner_pairs)
    col_outer = across(col_inner, outward)
    col_inner_far, col_outer = lax.optimization_barrier((col_inner_far, col_outer))
    (both,) = call(reduced_kernel, [(4, rank, rank)], [core, lent, probes, probes_far, pattern], "vvvvs")
    both_other = exchange(both, "step", 1)
    rows_scratch = [pltpu.VMEM((chips, 4, row_count, rank), jnp.float32), pltpu.SemaphoreType.DMA((2 * chips,))]
    y_parts = call(y_kernel, [(row_count, rank)] * chips, [target_left, left_other, both, both_other], "aavv", rows_scratch)
    y_rows = y_parts[0]
    for bit in range(1, chips):
        y_rows = y_rows + exchange(y_parts[bit], "step", 2 * bit)
    y_all = [y_rows] + [exchange(y_rows, "step", 2 * bit) for bit in range(1, chips)]
    _, col_last = lax.optimization_barrier((y_rows, col_inner_far))
    col_last = across(col_last, outward)
    (sent,) = call(z_kernel, [(5, rank, rank)], [target_left, left_other, *y_all], "aa" + "v" * chips, rows_scratch)
    got = exchange(sent, "step", 1)
    w_parts = call(
        functools.partial(w_kernel, planes),
        [(row_count, rank)] * planes,
        [sent, got, both, both_other, col_half, col_near, col_inner, col_inner_far, col_outer, col_last],
        "vvvvaaaaaa",
        [pltpu.VMEM((planes, 4, row_count, rank), jnp.float32), pltpu.SemaphoreType.DMA((planes,))],
    )
    w_got = [exchange(w_parts[bit], "step", 2 * bit) for bit in range(1, chips)]
    basis, inverse = call(
        functools.partial(basis_kernel, tile_rows, 32, 16), [(row_count, rank), (rank, rank)], [sent, got, y_rows], cost=10**9
    )
    (factor,) = call(functools.partial(factor_kernel, tile_rows), [(row_count, rank)], [w_parts[0], *w_got, inverse])
    return basis[None], factor[None]


def solution(mesh):
    line = mesh.shape["tile"] == 4 and mesh.shape["step"] == 8
    return jax.shard_map(
        local_line if line else local_general,
        mesh=mesh,
        in_specs=(
            P("step", "tile", None, None),
            P("step", "tile", None, None),
            P("step", "tile", None),
            P("step", "tile", None),
            P("tile", None),
            P("step", "tile"),
        ),
        out_specs=(P("tile", "step", None), P("tile", "step", None)),
        check_vma=False,
    )
```

```python
import functools

import jax
import jax.numpy as jnp
from jax import lax
from jax.experimental import pallas as pl
from jax.experimental.pallas import tpu as pltpu
from jax.sharding import PartitionSpec as P

HIGH = lax.Precision.HIGH


def mm(spec, *arrays):
    return jnp.einsum(spec, *arrays, precision=HIGH, preferred_element_type=jnp.float32)


def inverse_factor(gram):
    lower = jnp.linalg.cholesky(gram)
    eye = jnp.eye(gram.shape[-1], dtype=gram.dtype)
    return jax.scipy.linalg.solve_triangular(lower, eye, lower=True)


def exchange(array, axis, bit):
    return lax.ppermute(array, axis, [(i, i ^ bit) for i in range(lax.axis_size(axis))])


def take(array, index, axis):
    return lax.dynamic_index_in_dim(array, index, axis, keepdims=False)


def local_general(target_left, target_right, column_left, column_right, sketch, pattern):
    left, right = target_left[:, 0], target_right[:, 0]
    tile_rows = left.shape[1]
    probes = lax.psum(mm("kbq,bp->kqp", column_left, sketch), "tile")
    col_left = lax.all_gather(column_left, "tile", axis=1, tiled=True)
    col_right = lax.all_gather(column_right, "tile", axis=1, tiled=True)
    core = mm("kbr,kbq->krq", right, col_right) * pattern[:, 0].astype(jnp.float32)[:, None, None]
    reduced = mm("krq,kqp->krp", core, probes)
    sketched = lax.psum(mm("kbr,krp->bp", left, reduced), "step")
    inverse = inverse_factor(mm("bp,bq->pq", sketched, sketched) / tile_rows)
    row_count = tile_rows // lax.axis_size("step")
    rows = lax.dynamic_slice_in_dim(sketched, lax.axis_index("step") * row_count, row_count, 0)
    projected = mm("kbr,bp->krp", left, sketched)
    returned = mm("krq,krp->kqp", core, projected)
    partial = mm("kbq,kqp->bp", col_left, returned)
    factor = lax.psum_scatter(partial, "step", scatter_dimension=0, tiled=True) / tile_rows
    return mm("bp,qp->bq", rows, inverse)[None], mm("bp,qp->bq", factor, inverse)[None]


TN = (((0,), (0,)), ((), ()))
NN = (((1,), (0,)), ((), ()))
NT = (((1,), (1,)), ((), ()))


def split(array):
    high = array.astype(jnp.bfloat16)
    return high, (array - high.astype(jnp.float32)).astype(jnp.bfloat16)


def dot3(a, b, dims):
    a_high, a_low = split(a)
    b_high, b_low = split(b)
    axis = 1 - dims[0][1][0]
    width = b.shape[axis]
    dot = functools.partial(lax.dot_general, dimension_numbers=dims, preferred_element_type=jnp.float32)
    wide = dot(a_high, jnp.concatenate([b_high, b_low], axis))
    return wide[:, :width] + wide[:, width:] + dot(a_low, b_high)


def dot_full(a, b, dims):
    return lax.dot_general(a, b, dims, precision=lax.Precision.HIGHEST, preferred_element_type=jnp.float32)


def call(kernel, outs, args, spaces="", scratch=(), cost=0):
    kinds = {"v": pltpu.VMEM, "a": pl.ANY, "s": pltpu.SMEM}
    spaces = spaces or "v" * len(args)
    shapes = [jax.ShapeDtypeStruct(shape, jnp.float32) for shape in outs]
    return pl.pallas_call(
        kernel,
        out_shape=shapes,
        in_specs=[pl.BlockSpec(memory_space=kinds[letter]) for letter in spaces],
        out_specs=[pl.BlockSpec(memory_space=pltpu.VMEM) for _ in shapes],
        scratch_shapes=list(scratch),
        compiler_params=pltpu.CompilerParams(vmem_limit_bytes=24 << 20),
        cost_estimate=pl.CostEstimate(flops=cost, bytes_accessed=0, transcendentals=0),
    )(*args)


def core_kernel(planes, part, own_rows, first, second, core, lent):
    plane = lax.axis_index("tile")
    is_end = jnp.logical_or(plane == 0, plane == planes - 1)

    @pl.when(is_end)
    def _():
        for k in range(2):
            core[k] = part[k] + dot3(own_rows[k], second[k], TN)
            lent[k] = jnp.zeros_like(core[k])

    @pl.when(jnp.logical_not(is_end))
    def _():
        for k in range(2):
            core[k] = part[k] + dot3(own_rows[k], first[k], TN)
            lent[k] = dot3(second[k], first[k], TN)


def reduced_kernel(core, lent, probe_here, probe_far, pattern, both):
    for k in range(2):
        weight = pattern[k, 0].astype(jnp.float32)
        c = (core[k] + lent[k]) * weight
        both[k] = dot3(c, probe_here[k] + probe_far[k], NN)
        both[2 + k] = c


def start_rows(left, left_other, held, sems, chips, rows):
    position = lax.axis_index("step")
    chip, bit = position // 2, position % 2
    copies = []
    for i in range(chips):
        block = jnp.bitwise_xor(chip, i)
        mine = left.at[:, 0, pl.ds(pl.multiple_of((block * 2 + bit) * rows, rows), rows), :]
        copies.append((
            pltpu.make_async_copy(mine, held.at[i, pl.ds(0, 2)], sems.at[2 * i]),
            pltpu.make_async_copy(left_other.at[:, block], held.at[i, pl.ds(2, 2)], sems.at[2 * i + 1]),
        ))
    for pair in copies:
        for copy in pair:
            copy.start()
    return copies


def y_kernel(left, left_other, both, both_other, *rest):
    *outs, held, sems = rest
    chips, rows = len(outs), outs[0].shape[0]
    copies = start_rows(left, left_other, held, sems, chips, rows)
    reduced = jnp.concatenate([both[0], both[1], both_other[0], both_other[1]], 0)
    for i, out in enumerate(outs):
        for copy in copies[i]:
            copy.wait()
        out[...] = dot3(jnp.concatenate([held[i, k] for k in range(4)], 1), reduced, NN)


def z_kernel(left, left_other, *rest):
    *ys, out, held, sems = rest
    chips, rows = len(ys), ys[0].shape[0]
    rank = out.shape[-1]
    copies = start_rows(left, left_other, held, sems, chips, rows)
    total = jnp.zeros((rank, 5 * rank), jnp.float32)
    dot = functools.partial(lax.dot_general, dimension_numbers=TN, preferred_element_type=jnp.float32)
    for i, y in enumerate(ys):
        y_here = y[...]
        for copy in copies[i]:
            copy.wait()
        beside = jnp.concatenate([held[i, 2], held[i, 3], held[i, 0], held[i, 1], y_here], 1)
        b_high, b_low = split(beside)
        a_high, a_low = split(y_here)
        total += dot(a_high, b_high) + dot(a_high, b_low) + dot(a_low, b_high)
    for k in range(5):
        out[k] = total[:, k * rank:(k + 1) * rank]


def w_kernel(planes, sent, got, both, both_other, own, near, inner, inner_far, outer, last, *rest):
    *outs, held, sems = rest
    plane = lax.axis_index("tile")
    chip = lax.axis_index("step") // 2
    is_end = jnp.logical_or(plane == 0, plane == planes - 1)

    def pick(i, wanted, source):
        @pl.when(wanted)
        def _():
            pltpu.make_async_copy(source, held.at[i], sems.at[i]).start()

    for i in range(planes):
        block = jnp.bitwise_xor(chip, i)
        apart = jnp.bitwise_xor(block, plane)
        pick(i, apart == 0, own)
        pick(i, apart == 1, near)
        pick(i, jnp.logical_and(apart == 2, is_end), outer)
        pick(i, jnp.logical_and(apart == 2, jnp.logical_not(is_end)), inner_far)
        pick(i, jnp.logical_and(apart == 3, is_end), last)
        pick(i, jnp.logical_and(apart == 3, jnp.logical_not(is_end)), inner)
    returned = []
    for k in range(2):
        returned.append(dot3(sent[2 + k] + got[k], both[2 + k], NN))
    for k in range(2):
        returned.append(dot3(sent[k] + got[2 + k], both_other[2 + k], NN))
    returned = jnp.concatenate(returned, 1)
    for i, out in enumerate(outs):
        pltpu.make_async_copy(own, held.at[i], sems.at[i]).wait()
        out[...] = dot3(jnp.concatenate([held[i, k] for k in range(4)], 1), returned, NT)


def basis_kernel(tile_rows, width, group, sent, got, y_rows, basis, inverse):
    rank = inverse.shape[0]
    left = (sent[4] + got[4]) * (1.0 / tile_rows)
    index = lax.broadcasted_iota(jnp.int32, (rank, rank), 0)
    right = (index == lax.broadcasted_iota(jnp.int32, (rank, rank), 1)).astype(jnp.float32)
    row_index = lax.broadcasted_iota(jnp.int32, (width, rank), 0)
    done = []
    for begin in range(0, rank, width):
        l, r = left[:width], right[:width]
        scale = jnp.zeros((width, rank), jnp.float32)
        for first in range(0, width, group):
            place = begin + first
            columns = [jnp.broadcast_to(l[:, place + c:place + c + 1], (width, rank)) for c in range(group)]
            for c in range(group):
                j = first + c
                pivot = columns[c][j:j + 1]
                scale = jnp.where(row_index == j, lax.rsqrt(pivot), scale)
                factor = jnp.where(row_index > j, columns[c] * (1.0 / pivot), 0.0)
                for d in range(c + 1, group):
                    columns[d] = columns[d] - factor * columns[d][j:j + 1]
                l, r = l - factor * l[j:j + 1], r - factor * r[j:j + 1]
        l, r = l * scale, r * scale
        done.append(r)
        if begin + width < rank:
            both = dot_full(l[:, begin + width:], jnp.concatenate([l, r], 1), TN)
            left, right = left[width:] - both[:, :rank], right[width:] - both[:, rank:]
    lower_inverse = jnp.concatenate(done, 0)
    inverse[...] = lower_inverse
    basis[...] = dot_full(y_rows[...], lower_inverse, NT)


def factor_kernel(tile_rows, a, b, c, d, inverse, factor):
    total = (a[...] + b[...] + c[...] + d[...]) * (1.0 / tile_rows)
    factor[...] = dot_full(total, inverse[...], NT)


def local_line(target_left, target_right, column_left, column_right, sketch, pattern):
    tile_rows, rank = target_left.shape[2:]
    planes = lax.axis_size("tile")
    chips = lax.axis_size("step") // 2
    plane = lax.axis_index("tile")
    core_bit = lax.axis_index("step") % 2
    chip = lax.axis_index("step") // 2
    row_count = tile_rows // (2 * chips)
    is_end = jnp.logical_or(plane == 0, plane == planes - 1)
    outer_pairs, inner_pairs = [(0, 1), (1, 0), (2, 3), (3, 2)], [(1, 2), (2, 1)]
    outward = [(1, 0), (2, 3)]

    def across(array, pairs):
        return lax.ppermute(array, "tile", pairs)

    near = across(column_right, outer_pairs)
    inner = across(column_right, inner_pairs)
    probes = mm("kbq,bp->kqp", column_left, sketch)
    probes = probes + across(probes, outer_pairs)
    right_blocks = target_right.reshape(2, planes, -1, rank)

    def block(index):
        return take(right_blocks, index, 1)

    inner_far = across(near, inner_pairs)
    outer_rows = jnp.where(is_end, block(planes - 1 - plane), inner)
    outer = across(outer_rows, outer_pairs)
    part = (
        mm("kbr,kbq->krq", block(plane), column_right)
        + mm("kbr,kbq->krq", block(plane ^ 1), near)
        + mm("kbr,kbq->krq", block(jnp.where(is_end, plane, planes - 1 - plane)), inner)
    )
    _, probes_held = lax.optimization_barrier(((near, inner), probes))
    probes_far = exchange(probes_held, "tile", 2)
    core, lent = call(
        functools.partial(core_kernel, planes),
        [(2, rank, rank)] * 2,
        [part, block(plane ^ 2), inner_far, outer],
    )
    lent = across(lent, outward)

    left_split = target_left.reshape(2, chips, 2, row_count, rank)
    left_other = exchange(take(left_split, 1 - core_bit, 2), "step", 1)
    col_split = column_left.reshape(2, 2, row_count, rank)
    col_half = jnp.concatenate([take(col_split, core_bit, 1), exchange(take(col_split, 1 - core_bit, 1), "step", 1)])
    _, col_held = lax.optimization_barrier((near, col_half))
    col_near = across(col_held, outer_pairs)
    col_inner = across(col_held, inner_pairs)
    col_near, col_inner = lax.optimization_barrier((col_near, col_inner))
    col_inner_far = across(col_near, inner_pairs)
    col_outer = across(col_inner, outward)
    col_inner_far, col_outer = lax.optimization_barrier((col_inner_far, col_outer))
    (both,) = call(reduced_kernel, [(4, rank, rank)], [core, lent, probes, probes_far, pattern], "vvvvs")
    both_other = exchange(both, "step", 1)
    rows_scratch = [pltpu.VMEM((chips, 4, row_count, rank), jnp.float32), pltpu.SemaphoreType.DMA((2 * chips,))]
    y_parts = call(y_kernel, [(row_count, rank)] * chips, [target_left, left_other, both, both_other], "aavv", rows_scratch)
    y_rows = y_parts[0]
    for bit in range(1, chips):
        y_rows = y_rows + exchange(y_parts[bit], "step", 2 * bit)
    y_all = [y_rows] + [exchange(y_rows, "step", 2 * bit) for bit in range(1, chips)]
    _, col_last = lax.optimization_barrier((y_rows, col_inner_far))
    col_last = across(col_last, outward)
    (sent,) = call(z_kernel, [(5, rank, rank)], [target_left, left_other, *y_all], "aa" + "v" * chips, rows_scratch)
    got = exchange(sent, "step", 1)
    w_parts = call(
        functools.partial(w_kernel, planes),
        [(row_count, rank)] * planes,
        [sent, got, both, both_other, col_half, col_near, col_inner, col_inner_far, col_outer, col_last],
        "vvvvaaaaaa",
        [pltpu.VMEM((planes, 4, row_count, rank), jnp.float32), pltpu.SemaphoreType.DMA((planes,))],
    )
    w_got = [exchange(w_parts[bit], "step", 2 * bit) for bit in range(1, chips)]
    basis, inverse = call(
        functools.partial(basis_kernel, tile_rows, 32, 16), [(row_count, rank), (rank, rank)], [sent, got, y_rows], cost=10**9
    )
    (factor,) = call(functools.partial(factor_kernel, tile_rows), [(row_count, rank)], [w_parts[0], *w_got, inverse])
    return basis[None], factor[None]


def solution(mesh):
    line = mesh.shape["tile"] == 4 and mesh.shape["step"] == 8
    return jax.shard_map(
        local_line if line else local_general,
        mesh=mesh,
        in_specs=(
            P("step", "tile", None, None),
            P("step", "tile", None, None),
            P("step", "tile", None),
            P("step", "tile", None),
            P("tile", None),
            P("step", "tile"),
        ),
        out_specs=(P("tile", "step", None), P("tile", "step", None)),
        check_vma=False,
    )
```

```python
import functools

import jax
import jax.numpy as jnp
from jax import lax
from jax.experimental import pallas as pl
from jax.experimental.pallas import tpu as pltpu
from jax.sharding import PartitionSpec as P

HIGH = lax.Precision.HIGH


def mm(spec, *arrays):
    return jnp.einsum(spec, *arrays, precision=HIGH, preferred_element_type=jnp.float32)


def inverse_factor(gram):
    lower = jnp.linalg.cholesky(gram)
    eye = jnp.eye(gram.shape[-1], dtype=gram.dtype)
    return jax.scipy.linalg.solve_triangular(lower, eye, lower=True)


def exchange(array, axis, bit):
    return lax.ppermute(array, axis, [(i, i ^ bit) for i in range(lax.axis_size(axis))])


def take(array, index, axis):
    return lax.dynamic_index_in_dim(array, index, axis, keepdims=False)


def local_general(target_left, target_right, column_left, column_right, sketch, pattern):
    left, right = target_left[:, 0], target_right[:, 0]
    tile_rows = left.shape[1]
    probes = lax.psum(mm("kbq,bp->kqp", column_left, sketch), "tile")
    col_left = lax.all_gather(column_left, "tile", axis=1, tiled=True)
    col_right = lax.all_gather(column_right, "tile", axis=1, tiled=True)
    core = mm("kbr,kbq->krq", right, col_right) * pattern[:, 0].astype(jnp.float32)[:, None, None]
    reduced = mm("krq,kqp->krp", core, probes)
    sketched = lax.psum(mm("kbr,krp->bp", left, reduced), "step")
    inverse = inverse_factor(mm("bp,bq->pq", sketched, sketched) / tile_rows)
    row_count = tile_rows // lax.axis_size("step")
    rows = lax.dynamic_slice_in_dim(sketched, lax.axis_index("step") * row_count, row_count, 0)
    projected = mm("kbr,bp->krp", left, sketched)
    returned = mm("krq,krp->kqp", core, projected)
    partial = mm("kbq,kqp->bp", col_left, returned)
    factor = lax.psum_scatter(partial, "step", scatter_dimension=0, tiled=True) / tile_rows
    return mm("bp,qp->bq", rows, inverse)[None], mm("bp,qp->bq", factor, inverse)[None]


TN = (((0,), (0,)), ((), ()))
NN = (((1,), (0,)), ((), ()))
NT = (((1,), (1,)), ((), ()))


def split(array):
    high = array.astype(jnp.bfloat16)
    return high, (array - high.astype(jnp.float32)).astype(jnp.bfloat16)


def dot3(a, b, dims):
    a_high, a_low = split(a)
    b_high, b_low = split(b)
    axis = 1 - dims[0][1][0]
    width = b.shape[axis]
    dot = functools.partial(lax.dot_general, dimension_numbers=dims, preferred_element_type=jnp.float32)
    wide = dot(a_high, jnp.concatenate([b_high, b_low], axis))
    return wide[:, :width] + wide[:, width:] + dot(a_low, b_high)


def dot_full(a, b, dims):
    return lax.dot_general(a, b, dims, precision=lax.Precision.HIGHEST, preferred_element_type=jnp.float32)


def call(kernel, outs, args, spaces="", scratch=(), cost=0):
    kinds = {"v": pltpu.VMEM, "a": pl.ANY, "s": pltpu.SMEM}
    spaces = spaces or "v" * len(args)
    shapes = [jax.ShapeDtypeStruct(shape, jnp.float32) for shape in outs]
    return pl.pallas_call(
        kernel,
        out_shape=shapes,
        in_specs=[pl.BlockSpec(memory_space=kinds[letter]) for letter in spaces],
        out_specs=[pl.BlockSpec(memory_space=pltpu.VMEM) for _ in shapes],
        scratch_shapes=list(scratch),
        compiler_params=pltpu.CompilerParams(vmem_limit_bytes=24 << 20),
        cost_estimate=pl.CostEstimate(flops=cost, bytes_accessed=0, transcendentals=0),
    )(*args)


def core_kernel(planes, part, own_rows, first, second, probe_far, core, lent):
    lent[pl.ds(2, 2)] = probe_far[...]
    plane = lax.axis_index("tile")
    is_end = jnp.logical_or(plane == 0, plane == planes - 1)

    @pl.when(is_end)
    def _():
        for k in range(2):
            core[k] = part[k] + dot3(own_rows[k], second[k], TN)
            lent[k] = jnp.zeros_like(core[k])

    @pl.when(jnp.logical_not(is_end))
    def _():
        for k in range(2):
            core[k] = part[k] + dot3(own_rows[k], first[k], TN)
            lent[k] = dot3(second[k], first[k], TN)


def reduced_kernel(core, lent, probe_here, probe_far, pattern, both):
    for k in range(2):
        weight = pattern[k, 0].astype(jnp.float32)
        c = (core[k] + lent[k]) * weight
        both[k] = dot3(c, probe_here[k] + probe_far[k] + lent[2 + k], NN)
        both[2 + k] = c


def start_rows(left, left_other, held, sems, chips, rows):
    position = lax.axis_index("step")
    chip, bit = position // 2, position % 2
    copies = []
    for i in range(chips):
        block = jnp.bitwise_xor(chip, i)
        mine = left.at[:, 0, pl.ds(pl.multiple_of((block * 2 + bit) * rows, rows), rows), :]
        copies.append((
            pltpu.make_async_copy(mine, held.at[i, pl.ds(0, 2)], sems.at[2 * i]),
            pltpu.make_async_copy(left_other.at[:, block], held.at[i, pl.ds(2, 2)], sems.at[2 * i + 1]),
        ))
    for pair in copies:
        for copy in pair:
            copy.start()
    return copies


def y_kernel(left, left_other, both, both_other, *rest):
    *outs, held, sems = rest
    chips, rows = len(outs), outs[0].shape[0]
    copies = start_rows(left, left_other, held, sems, chips, rows)
    reduced = jnp.concatenate([both[0], both[1], both_other[0], both_other[1]], 0)
    for i, out in enumerate(outs):
        for copy in copies[i]:
            copy.wait()
        out[...] = dot3(jnp.concatenate([held[i, k] for k in range(4)], 1), reduced, NN)


def z_kernel(left, left_other, *rest):
    *ys, out, held, sems = rest
    chips, rows = len(ys), ys[0].shape[0]
    rank = out.shape[-1]
    copies = start_rows(left, left_other, held, sems, chips, rows)
    total = jnp.zeros((rank, 5 * rank), jnp.float32)
    dot = functools.partial(lax.dot_general, dimension_numbers=TN, preferred_element_type=jnp.float32)
    for i, y in enumerate(ys):
        y_here = y[...]
        for copy in copies[i]:
            copy.wait()
        beside = jnp.concatenate([held[i, 2], held[i, 3], held[i, 0], held[i, 1], y_here], 1)
        b_high, b_low = split(beside)
        a_high, a_low = split(y_here)
        total += dot(a_high, b_high) + dot(a_high, b_low) + dot(a_low, b_high)
    for k in range(5):
        out[k] = total[:, k * rank:(k + 1) * rank]


def w_kernel(planes, sent, got, both, both_other, own, near, inner, inner_far, outer, last, *rest):
    *outs, held, sems = rest
    plane = lax.axis_index("tile")
    chip = lax.axis_index("step") // 2
    is_end = jnp.logical_or(plane == 0, plane == planes - 1)

    def pick(i, wanted, source):
        @pl.when(wanted)
        def _():
            pltpu.make_async_copy(source, held.at[i], sems.at[i]).start()

    for i in range(planes):
        block = jnp.bitwise_xor(chip, i)
        apart = jnp.bitwise_xor(block, plane)
        pick(i, apart == 0, own)
        pick(i, apart == 1, near)
        pick(i, jnp.logical_and(apart == 2, is_end), outer)
        pick(i, jnp.logical_and(apart == 2, jnp.logical_not(is_end)), inner_far)
        pick(i, jnp.logical_and(apart == 3, is_end), last)
        pick(i, jnp.logical_and(apart == 3, jnp.logical_not(is_end)), inner)
    returned = []
    for k in range(2):
        returned.append(dot3(sent[2 + k] + got[k], both[2 + k], NN))
    for k in range(2):
        returned.append(dot3(sent[k] + got[2 + k], both_other[2 + k], NN))
    returned = jnp.concatenate(returned, 1)
    for i, out in enumerate(outs):
        pltpu.make_async_copy(own, held.at[i], sems.at[i]).wait()
        out[...] = dot3(jnp.concatenate([held[i, k] for k in range(4)], 1), returned, NT)


def basis_kernel(tile_rows, width, group, sent, got, y_rows, basis, inverse):
    rank = inverse.shape[0]
    left = (sent[4] + got[4]) * (1.0 / tile_rows)
    index = lax.broadcasted_iota(jnp.int32, (rank, rank), 0)
    right = (index == lax.broadcasted_iota(jnp.int32, (rank, rank), 1)).astype(jnp.float32)
    row_index = lax.broadcasted_iota(jnp.int32, (width, rank), 0)
    done = []
    for begin in range(0, rank, width):
        l, r = left[:width], right[:width]
        scale = jnp.zeros((width, rank), jnp.float32)
        for first in range(0, width, group):
            place = begin + first
            columns = [jnp.broadcast_to(l[:, place + c:place + c + 1], (width, rank)) for c in range(group)]
            for c in range(group):
                j = first + c
                pivot = columns[c][j:j + 1]
                scale = jnp.where(row_index == j, lax.rsqrt(pivot), scale)
                factor = jnp.where(row_index > j, columns[c] * (1.0 / pivot), 0.0)
                for d in range(c + 1, group):
                    columns[d] = columns[d] - factor * columns[d][j:j + 1]
                l, r = l - factor * l[j:j + 1], r - factor * r[j:j + 1]
        l, r = l * scale, r * scale
        done.append(r)
        if begin + width < rank:
            both = dot_full(l[:, begin + width:], jnp.concatenate([l, r], 1), TN)
            left, right = left[width:] - both[:, :rank], right[width:] - both[:, rank:]
    lower_inverse = jnp.concatenate(done, 0)
    inverse[...] = lower_inverse
    basis[...] = dot_full(y_rows[...], lower_inverse, NT)


def factor_kernel(tile_rows, a, b, c, d, inverse, factor):
    total = (a[...] + b[...] + c[...] + d[...]) * (1.0 / tile_rows)
    factor[...] = dot_full(total, inverse[...], NT)


def local_line(target_left, target_right, column_left, column_right, sketch, pattern):
    tile_rows, rank = target_left.shape[2:]
    planes = lax.axis_size("tile")
    chips = lax.axis_size("step") // 2
    plane = lax.axis_index("tile")
    core_bit = lax.axis_index("step") % 2
    chip = lax.axis_index("step") // 2
    row_count = tile_rows // (2 * chips)
    is_end = jnp.logical_or(plane == 0, plane == planes - 1)
    outer_pairs, inner_pairs = [(0, 1), (1, 0), (2, 3), (3, 2)], [(1, 2), (2, 1)]
    outward = [(1, 0), (2, 3)]

    def across(array, pairs):
        return lax.ppermute(array, "tile", pairs)

    near = across(column_right, outer_pairs)
    inner = across(column_right, inner_pairs)
    probes = mm("kbq,bp->kqp", column_left, sketch)
    probes = probes + across(probes, outer_pairs)
    right_blocks = target_right.reshape(2, planes, -1, rank)

    def block(index):
        return take(right_blocks, index, 1)

    inner_far = across(near, inner_pairs)
    outer = across(jnp.where(is_end, block(planes - 1 - plane), inner), outer_pairs)
    part = (
        mm("kbr,kbq->krq", block(plane), column_right)
        + mm("kbr,kbq->krq", block(plane ^ 1), near)
        + mm("kbr,kbq->krq", block(jnp.where(is_end, plane, planes - 1 - plane)), inner)
    )
    _, probes_held = lax.optimization_barrier((near, probes))
    probes_far = across(probes_held, inner_pairs)
    far_rows = block(plane ^ 2)
    core, lent = call(functools.partial(core_kernel, planes), [(2, rank, rank), (4, rank, rank)], [part, far_rows, inner_far, outer, probes_far])
    lent = across(lent, outward)

    left_split = target_left.reshape(2, chips, 2, row_count, rank)
    left_other = exchange(take(left_split, 1 - core_bit, 2), "step", 1)
    col_split = column_left.reshape(2, 2, row_count, rank)
    col_half = jnp.concatenate([take(col_split, core_bit, 1), exchange(take(col_split, 1 - core_bit, 1), "step", 1)])
    _, col_held = lax.optimization_barrier((near, col_half))
    col_near = across(col_held, outer_pairs)
    col_inner = across(col_held, inner_pairs)
    col_near, col_inner = lax.optimization_barrier((col_near, col_inner))
    col_inner_far = across(col_near, inner_pairs)
    col_outer = across(col_inner, outward)
    col_inner_far, col_outer = lax.optimization_barrier((col_inner_far, col_outer))
    (both,) = call(reduced_kernel, [(4, rank, rank)], [core, lent, probes, probes_far, pattern], "vvvvs")
    both_other = exchange(both, "step", 1)
    rows_scratch = [pltpu.VMEM((chips, 4, row_count, rank), jnp.float32), pltpu.SemaphoreType.DMA((2 * chips,))]
    y_parts = call(y_kernel, [(row_count, rank)] * chips, [target_left, left_other, both, both_other], "aavv", rows_scratch)
    y_rows = y_parts[0]
    for bit in range(1, chips):
        y_rows = y_rows + exchange(y_parts[bit], "step", 2 * bit)
    y_all = [y_rows] + [exchange(y_rows, "step", 2 * bit) for bit in range(1, chips)]
    col_last = across(col_inner_far, outward)
    (sent,) = call(z_kernel, [(5, rank, rank)], [target_left, left_other, *y_all], "aa" + "v" * chips, rows_scratch)
    got = exchange(sent, "step", 1)
    w_parts = call(
        functools.partial(w_kernel, planes),
        [(row_count, rank)] * planes,
        [sent, got, both, both_other, col_half, col_near, col_inner, col_inner_far, col_outer, col_last],
        "vvvvaaaaaa",
        [pltpu.VMEM((planes, 4, row_count, rank), jnp.float32), pltpu.SemaphoreType.DMA((planes,))],
    )
    w_got = [exchange(w_parts[bit], "step", 2 * bit) for bit in range(1, chips)]
    basis, inverse = call(
        functools.partial(basis_kernel, tile_rows, 32, 16), [(row_count, rank), (rank, rank)], [sent, got, y_rows], cost=10**9
    )
    (factor,) = call(functools.partial(factor_kernel, tile_rows), [(row_count, rank)], [w_parts[0], *w_got, inverse])
    return basis[None], factor[None]


def solution(mesh):
    line = mesh.shape["tile"] == 4 and mesh.shape["step"] == 8
    return jax.shard_map(
        local_line if line else local_general,
        mesh=mesh,
        in_specs=(
            P("step", "tile", None, None),
            P("step", "tile", None, None),
            P("step", "tile", None),
            P("step", "tile", None),
            P("tile", None),
            P("step", "tile"),
        ),
        out_specs=(P("tile", "step", None), P("tile", "step", None)),
        check_vma=False,
    )
```

```python
import functools

import jax
import jax.numpy as jnp
from jax import lax
from jax.experimental import pallas as pl
from jax.experimental.pallas import tpu as pltpu
from jax.sharding import PartitionSpec as P

HIGH = lax.Precision.HIGH


def mm(spec, *arrays):
    return jnp.einsum(spec, *arrays, precision=HIGH, preferred_element_type=jnp.float32)


def inverse_factor(gram):
    lower = jnp.linalg.cholesky(gram)
    eye = jnp.eye(gram.shape[-1], dtype=gram.dtype)
    return jax.scipy.linalg.solve_triangular(lower, eye, lower=True)


def exchange(array, axis, bit):
    return lax.ppermute(array, axis, [(i, i ^ bit) for i in range(lax.axis_size(axis))])


def take(array, index, axis):
    return lax.dynamic_index_in_dim(array, index, axis, keepdims=False)


def local_general(target_left, target_right, column_left, column_right, sketch, pattern):
    left, right = target_left[:, 0], target_right[:, 0]
    tile_rows = left.shape[1]
    probes = lax.psum(mm("kbq,bp->kqp", column_left, sketch), "tile")
    col_left = lax.all_gather(column_left, "tile", axis=1, tiled=True)
    col_right = lax.all_gather(column_right, "tile", axis=1, tiled=True)
    core = mm("kbr,kbq->krq", right, col_right) * pattern[:, 0].astype(jnp.float32)[:, None, None]
    reduced = mm("krq,kqp->krp", core, probes)
    sketched = lax.psum(mm("kbr,krp->bp", left, reduced), "step")
    inverse = inverse_factor(mm("bp,bq->pq", sketched, sketched) / tile_rows)
    row_count = tile_rows // lax.axis_size("step")
    rows = lax.dynamic_slice_in_dim(sketched, lax.axis_index("step") * row_count, row_count, 0)
    projected = mm("kbr,bp->krp", left, sketched)
    returned = mm("krq,krp->kqp", core, projected)
    partial = mm("kbq,kqp->bp", col_left, returned)
    factor = lax.psum_scatter(partial, "step", scatter_dimension=0, tiled=True) / tile_rows
    return mm("bp,qp->bq", rows, inverse)[None], mm("bp,qp->bq", factor, inverse)[None]


TN = (((0,), (0,)), ((), ()))
NN = (((1,), (0,)), ((), ()))
NT = (((1,), (1,)), ((), ()))


def split(array):
    high = array.astype(jnp.bfloat16)
    return high, (array - high.astype(jnp.float32)).astype(jnp.bfloat16)


def dot3(a, b, dims):
    a_high, a_low = split(a)
    b_high, b_low = split(b)
    axis = 1 - dims[0][1][0]
    width = b.shape[axis]
    dot = functools.partial(lax.dot_general, dimension_numbers=dims, preferred_element_type=jnp.float32)
    wide = dot(a_high, jnp.concatenate([b_high, b_low], axis))
    return wide[:, :width] + wide[:, width:] + dot(a_low, b_high)


def dot_full(a, b, dims):
    return lax.dot_general(a, b, dims, precision=lax.Precision.HIGHEST, preferred_element_type=jnp.float32)


def call(kernel, outs, args, spaces="", scratch=(), cost=0):
    kinds = {"v": pltpu.VMEM, "a": pl.ANY, "s": pltpu.SMEM}
    spaces = spaces or "v" * len(args)
    shapes = [jax.ShapeDtypeStruct(shape, jnp.float32) for shape in outs]
    return pl.pallas_call(
        kernel,
        out_shape=shapes,
        in_specs=[pl.BlockSpec(memory_space=kinds[letter]) for letter in spaces],
        out_specs=[pl.BlockSpec(memory_space=pltpu.VMEM) for _ in shapes],
        scratch_shapes=list(scratch),
        compiler_params=pltpu.CompilerParams(vmem_limit_bytes=24 << 20),
        cost_estimate=pl.CostEstimate(flops=cost, bytes_accessed=0, transcendentals=0),
    )(*args)


def lent_kernel(planes, first, second, lent):
    plane = lax.axis_index("tile")
    is_end = jnp.logical_or(plane == 0, plane == planes - 1)

    @pl.when(is_end)
    def _():
        for k in range(2):
            lent[k] = jnp.zeros(lent.shape[1:], jnp.float32)

    @pl.when(jnp.logical_not(is_end))
    def _():
        for k in range(2):
            lent[k] = dot3(second[k], first[k], TN)


def core_kernel(planes, part, right, first, second, core):
    plane = lax.axis_index("tile")
    rows = first.shape[1]
    far = pl.ds(pl.multiple_of(jnp.bitwise_xor(plane, 2) * rows, rows), rows)
    is_end = jnp.logical_or(plane == 0, plane == planes - 1)

    @pl.when(is_end)
    def _():
        for k in range(2):
            core[k] = part[k] + dot3(right[k, 0, far, :], second[k], TN)

    @pl.when(jnp.logical_not(is_end))
    def _():
        for k in range(2):
            core[k] = part[k] + dot3(right[k, 0, far, :], first[k], TN)


def reduced_kernel(core, lent, probe_here, probe_far, pattern, both):
    for k in range(2):
        weight = pattern[k, 0].astype(jnp.float32)
        c = (core[k] + lent[k]) * weight
        both[k] = dot3(c, probe_here[k] + probe_far[k], NN)
        both[2 + k] = c


def start_rows(left, left_other, held, sems, chips, rows):
    position = lax.axis_index("step")
    chip, bit = position // 2, position % 2
    copies = []
    for i in range(chips):
        block = jnp.bitwise_xor(chip, i)
        mine = left.at[:, 0, pl.ds(pl.multiple_of((block * 2 + bit) * rows, rows), rows), :]
        copies.append((
            pltpu.make_async_copy(mine, held.at[i, pl.ds(0, 2)], sems.at[2 * i]),
            pltpu.make_async_copy(left_other.at[:, block], held.at[i, pl.ds(2, 2)], sems.at[2 * i + 1]),
        ))
    for pair in copies:
        for copy in pair:
            copy.start()
    return copies


def y_kernel(left, left_other, both, both_other, *rest):
    *outs, held, sems = rest
    chips, rows = len(outs), outs[0].shape[0]
    copies = start_rows(left, left_other, held, sems, chips, rows)
    reduced = jnp.concatenate([both[0], both[1], both_other[0], both_other[1]], 0)
    for i, out in enumerate(outs):
        for copy in copies[i]:
            copy.wait()
        out[...] = dot3(jnp.concatenate([held[i, k] for k in range(4)], 1), reduced, NN)


def z_kernel(left, left_other, *rest):
    *ys, out, held, sems = rest
    chips, rows = len(ys), ys[0].shape[0]
    rank = out.shape[-1]
    copies = start_rows(left, left_other, held, sems, chips, rows)
    total = jnp.zeros((rank, 5 * rank), jnp.float32)
    dot = functools.partial(lax.dot_general, dimension_numbers=TN, preferred_element_type=jnp.float32)
    for i, y in enumerate(ys):
        y_here = y[...]
        for copy in copies[i]:
            copy.wait()
        beside = jnp.concatenate([held[i, 2], held[i, 3], held[i, 0], held[i, 1], y_here], 1)
        b_high, b_low = split(beside)
        a_high, a_low = split(y_here)
        total += dot(a_high, b_high) + dot(a_high, b_low) + dot(a_low, b_high)
    for k in range(5):
        out[k] = total[:, k * rank:(k + 1) * rank]


def w_kernel(planes, sent, got, both, both_other, own, near, inner, inner_far, outer, last, *rest):
    *outs, held, sems = rest
    plane = lax.axis_index("tile")
    chip = lax.axis_index("step") // 2
    is_end = jnp.logical_or(plane == 0, plane == planes - 1)

    def pick(i, wanted, source):
        @pl.when(wanted)
        def _():
            pltpu.make_async_copy(source, held.at[i], sems.at[i]).start()

    for i in range(planes):
        block = jnp.bitwise_xor(chip, i)
        apart = jnp.bitwise_xor(block, plane)
        pick(i, apart == 0, own)
        pick(i, apart == 1, near)
        pick(i, jnp.logical_and(apart == 2, is_end), outer)
        pick(i, jnp.logical_and(apart == 2, jnp.logical_not(is_end)), inner_far)
        pick(i, jnp.logical_and(apart == 3, is_end), last)
        pick(i, jnp.logical_and(apart == 3, jnp.logical_not(is_end)), inner)
    returned = []
    for k in range(2):
        returned.append(dot3(sent[2 + k] + got[k], both[2 + k], NN))
    for k in range(2):
        returned.append(dot3(sent[k] + got[2 + k], both_other[2 + k], NN))
    returned = jnp.concatenate(returned, 1)
    for i, out in enumerate(outs):
        pltpu.make_async_copy(own, held.at[i], sems.at[i]).wait()
        out[...] = dot3(jnp.concatenate([held[i, k] for k in range(4)], 1), returned, NT)


def basis_kernel(tile_rows, width, group, sent, got, y_rows, basis, inverse):
    rank = inverse.shape[0]
    left = (sent[4] + got[4]) * (1.0 / tile_rows)
    index = lax.broadcasted_iota(jnp.int32, (rank, rank), 0)
    right = (index == lax.broadcasted_iota(jnp.int32, (rank, rank), 1)).astype(jnp.float32)
    row_index = lax.broadcasted_iota(jnp.int32, (width, rank), 0)
    done = []
    for begin in range(0, rank, width):
        l, r = left[:width], right[:width]
        scale = jnp.zeros((width, rank), jnp.float32)
        for first in range(0, width, group):
            place = begin + first
            columns = [jnp.broadcast_to(l[:, place + c:place + c + 1], (width, rank)) for c in range(group)]
            for c in range(group):
                j = first + c
                pivot = columns[c][j:j + 1]
                scale = jnp.where(row_index == j, lax.rsqrt(pivot), scale)
                factor = jnp.where(row_index > j, columns[c] * (1.0 / pivot), 0.0)
                for d in range(c + 1, group):
                    columns[d] = columns[d] - factor * columns[d][j:j + 1]
                l, r = l - factor * l[j:j + 1], r - factor * r[j:j + 1]
        l, r = l * scale, r * scale
        done.append(r)
        if begin + width < rank:
            both = dot_full(l[:, begin + width:], jnp.concatenate([l, r], 1), TN)
            left, right = left[width:] - both[:, :rank], right[width:] - both[:, rank:]
    lower_inverse = jnp.concatenate(done, 0)
    inverse[...] = lower_inverse
    basis[...] = dot_full(y_rows[...], lower_inverse, NT)


def factor_kernel(tile_rows, a, b, c, d, inverse, factor):
    total = (a[...] + b[...] + c[...] + d[...]) * (1.0 / tile_rows)
    factor[...] = dot_full(total, inverse[...], NT)


def local_line(target_left, target_right, column_left, column_right, sketch, pattern):
    tile_rows, rank = target_left.shape[2:]
    planes = lax.axis_size("tile")
    chips = lax.axis_size("step") // 2
    plane = lax.axis_index("tile")
    core_bit = lax.axis_index("step") % 2
    chip = lax.axis_index("step") // 2
    row_count = tile_rows // (2 * chips)
    is_end = jnp.logical_or(plane == 0, plane == planes - 1)
    outer_pairs, inner_pairs = [(0, 1), (1, 0), (2, 3), (3, 2)], [(1, 2), (2, 1)]
    outward = [(1, 0), (2, 3)]

    def across(array, pairs):
        return lax.ppermute(array, "tile", pairs)

    near = across(column_right, outer_pairs)
    inner = across(column_right, inner_pairs)
    probes = mm("kbq,bp->kqp", column_left, sketch)
    probes = probes + across(probes, outer_pairs)
    near, inner = lax.optimization_barrier((near, inner))
    right_blocks = target_right.reshape(2, planes, -1, rank)

    def block(index):
        return take(right_blocks, index, 1)

    inner_far = across(near, inner_pairs)
    outer_rows = jnp.where(is_end, block(planes - 1 - plane), inner)
    outer = across(outer_rows, outer_pairs)
    part = (
        mm("kbr,kbq->krq", block(plane), column_right)
        + mm("kbr,kbq->krq", block(plane ^ 1), near)
        + mm("kbr,kbq->krq", block(jnp.where(is_end, plane, planes - 1 - plane)), inner)
    )
    _, probes_held = lax.optimization_barrier(((near, inner), probes))
    probes_far = exchange(probes_held, "tile", 2)
    (lent,) = call(functools.partial(lent_kernel, planes), [(2, rank, rank)], [inner_far, outer])
    (core,) = call(functools.partial(core_kernel, planes), [(2, rank, rank)], [part, target_right, inner_far, outer])
    lent = across(lent, outward)

    left_split = target_left.reshape(2, chips, 2, row_count, rank)
    left_other = exchange(take(left_split, 1 - core_bit, 2), "step", 1)
    col_split = column_left.reshape(2, 2, row_count, rank)
    col_half = jnp.concatenate([take(col_split, core_bit, 1), exchange(take(col_split, 1 - core_bit, 1), "step", 1)])
    _, col_held = lax.optimization_barrier((part, col_half))
    col_near = across(col_held, outer_pairs)
    col_inner = across(col_held, inner_pairs)
    (both,) = call(reduced_kernel, [(4, rank, rank)], [core, lent, probes, probes_far, pattern], "vvvvs")
    _, near_held, inner_held = lax.optimization_barrier((both, col_near, col_inner))
    col_inner_far = across(near_held, inner_pairs)
    col_outer = across(inner_held, outward)
    col_inner_far, col_outer = lax.optimization_barrier((col_inner_far, col_outer))
    both_other = exchange(both, "step", 1)
    rows_scratch = [pltpu.VMEM((chips, 4, row_count, rank), jnp.float32), pltpu.SemaphoreType.DMA((2 * chips,))]
    y_parts = call(y_kernel, [(row_count, rank)] * chips, [target_left, left_other, both, both_other], "aavv", rows_scratch)
    y_rows = y_parts[0]
    for bit in range(1, chips):
        y_rows = y_rows + exchange(y_parts[bit], "step", 2 * bit)
    y_all = [y_rows] + [exchange(y_rows, "step", 2 * bit) for bit in range(1, chips)]
    col_last = across(col_inner_far, outward)
    (sent,) = call(z_kernel, [(5, rank, rank)], [target_left, left_other, *y_all], "aa" + "v" * chips, rows_scratch)
    got = exchange(sent, "step", 1)
    w_parts = call(
        functools.partial(w_kernel, planes),
        [(row_count, rank)] * planes,
        [sent, got, both, both_other, col_half, col_near, col_inner, col_inner_far, col_outer, col_last],
        "vvvvaaaaaa",
        [pltpu.VMEM((planes, 4, row_count, rank), jnp.float32), pltpu.SemaphoreType.DMA((planes,))],
    )
    w_got = [exchange(w_parts[bit], "step", 2 * bit) for bit in range(1, chips)]
    basis, inverse = call(
        functools.partial(basis_kernel, tile_rows, 32, 16), [(row_count, rank), (rank, rank)], [sent, got, y_rows], cost=10**9
    )
    (factor,) = call(functools.partial(factor_kernel, tile_rows), [(row_count, rank)], [w_parts[0], *w_got, inverse])
    return basis[None], factor[None]


def solution(mesh):
    line = mesh.shape["tile"] == 4 and mesh.shape["step"] == 8
    return jax.shard_map(
        local_line if line else local_general,
        mesh=mesh,
        in_specs=(
            P("step", "tile", None, None),
            P("step", "tile", None, None),
            P("step", "tile", None),
            P("step", "tile", None),
            P("tile", None),
            P("step", "tile"),
        ),
        out_specs=(P("tile", "step", None), P("tile", "step", None)),
        check_vma=False,
    )
```

```python
import functools

import jax
import jax.numpy as jnp
from jax import lax
from jax.experimental import pallas as pl
from jax.experimental.pallas import tpu as pltpu
from jax.sharding import PartitionSpec as P

HIGH = lax.Precision.HIGH


def mm(spec, *arrays):
    return jnp.einsum(spec, *arrays, precision=HIGH, preferred_element_type=jnp.float32)


def inverse_factor(gram):
    lower = jnp.linalg.cholesky(gram)
    eye = jnp.eye(gram.shape[-1], dtype=gram.dtype)
    return jax.scipy.linalg.solve_triangular(lower, eye, lower=True)


def exchange(array, axis, bit):
    return lax.ppermute(array, axis, [(i, i ^ bit) for i in range(lax.axis_size(axis))])


def take(array, index, axis):
    return lax.dynamic_index_in_dim(array, index, axis, keepdims=False)


def local_general(target_left, target_right, column_left, column_right, sketch, pattern):
    left, right = target_left[:, 0], target_right[:, 0]
    tile_rows = left.shape[1]
    probes = lax.psum(mm("kbq,bp->kqp", column_left, sketch), "tile")
    col_left = lax.all_gather(column_left, "tile", axis=1, tiled=True)
    col_right = lax.all_gather(column_right, "tile", axis=1, tiled=True)
    core = mm("kbr,kbq->krq", right, col_right) * pattern[:, 0].astype(jnp.float32)[:, None, None]
    reduced = mm("krq,kqp->krp", core, probes)
    sketched = lax.psum(mm("kbr,krp->bp", left, reduced), "step")
    inverse = inverse_factor(mm("bp,bq->pq", sketched, sketched) / tile_rows)
    row_count = tile_rows // lax.axis_size("step")
    rows = lax.dynamic_slice_in_dim(sketched, lax.axis_index("step") * row_count, row_count, 0)
    projected = mm("kbr,bp->krp", left, sketched)
    returned = mm("krq,krp->kqp", core, projected)
    partial = mm("kbq,kqp->bp", col_left, returned)
    factor = lax.psum_scatter(partial, "step", scatter_dimension=0, tiled=True) / tile_rows
    return mm("bp,qp->bq", rows, inverse)[None], mm("bp,qp->bq", factor, inverse)[None]


TN = (((0,), (0,)), ((), ()))
NN = (((1,), (0,)), ((), ()))
NT = (((1,), (1,)), ((), ()))


def split(array):
    high = array.astype(jnp.bfloat16)
    return high, (array - high.astype(jnp.float32)).astype(jnp.bfloat16)


def dot3(a, b, dims):
    a_high, a_low = split(a)
    b_high, b_low = split(b)
    axis = 1 - dims[0][1][0]
    width = b.shape[axis]
    dot = functools.partial(lax.dot_general, dimension_numbers=dims, preferred_element_type=jnp.float32)
    wide = dot(a_high, jnp.concatenate([b_high, b_low], axis))
    return wide[:, :width] + wide[:, width:] + dot(a_low, b_high)


def dot_full(a, b, dims):
    return lax.dot_general(a, b, dims, precision=lax.Precision.HIGHEST, preferred_element_type=jnp.float32)


def call(kernel, outs, args, spaces="", scratch=(), cost=0):
    kinds = {"v": pltpu.VMEM, "a": pl.ANY, "s": pltpu.SMEM}
    spaces = spaces or "v" * len(args)
    shapes = [jax.ShapeDtypeStruct(shape, jnp.float32) for shape in outs]
    return pl.pallas_call(
        kernel,
        out_shape=shapes,
        in_specs=[pl.BlockSpec(memory_space=kinds[letter]) for letter in spaces],
        out_specs=[pl.BlockSpec(memory_space=pltpu.VMEM) for _ in shapes],
        scratch_shapes=list(scratch),
        compiler_params=pltpu.CompilerParams(vmem_limit_bytes=24 << 20),
        cost_estimate=pl.CostEstimate(flops=cost, bytes_accessed=0, transcendentals=0),
    )(*args)


def lent_kernel(planes, first, second, lent):
    plane = lax.axis_index("tile")
    is_end = jnp.logical_or(plane == 0, plane == planes - 1)

    @pl.when(is_end)
    def _():
        for k in range(2):
            lent[k] = jnp.zeros(lent.shape[1:], jnp.float32)

    @pl.when(jnp.logical_not(is_end))
    def _():
        for k in range(2):
            lent[k] = dot3(second[k], first[k], TN)


def core_kernel(planes, part, right, first, second, core):
    plane = lax.axis_index("tile")
    rows = first.shape[1]
    far = pl.ds(pl.multiple_of(jnp.bitwise_xor(plane, 2) * rows, rows), rows)
    is_end = jnp.logical_or(plane == 0, plane == planes - 1)

    @pl.when(is_end)
    def _():
        for k in range(2):
            core[k] = part[k] + dot3(right[k, 0, far, :], second[k], TN)

    @pl.when(jnp.logical_not(is_end))
    def _():
        for k in range(2):
            core[k] = part[k] + dot3(right[k, 0, far, :], first[k], TN)


def reduced_kernel(core, lent, probe_here, probe_far, pattern, both):
    for k in range(2):
        weight = pattern[k, 0].astype(jnp.float32)
        c = (core[k] + lent[k]) * weight
        both[k] = dot3(c, probe_here[k] + probe_far[k], NN)
        both[2 + k] = c


def start_rows(left, left_other, held, sems, chips, rows):
    position = lax.axis_index("step")
    chip, bit = position // 2, position % 2
    copies = []
    for i in range(chips):
        block = jnp.bitwise_xor(chip, i)
        mine = left.at[:, 0, pl.ds(pl.multiple_of((block * 2 + bit) * rows, rows), rows), :]
        copies.append((
            pltpu.make_async_copy(mine, held.at[i, pl.ds(0, 2)], sems.at[2 * i]),
            pltpu.make_async_copy(left_other.at[:, block], held.at[i, pl.ds(2, 2)], sems.at[2 * i + 1]),
        ))
    for pair in copies:
        for copy in pair:
            copy.start()
    return copies


def y_kernel(left, left_other, both, both_other, *rest):
    *outs, held, sems = rest
    chips, rows = len(outs), outs[0].shape[0]
    copies = start_rows(left, left_other, held, sems, chips, rows)
    reduced = jnp.concatenate([both[0], both[1], both_other[0], both_other[1]], 0)
    for i, out in enumerate(outs):
        for copy in copies[i]:
            copy.wait()
        out[...] = dot3(jnp.concatenate([held[i, k] for k in range(4)], 1), reduced, NN)


def z_kernel(left, left_other, *rest):
    *ys, before, out, held, sems = rest
    rows = ys[0].shape[0]
    rank = out.shape[-1]
    copies = start_rows(left, left_other, held, sems, len(ys) + 1, rows)
    total = jnp.concatenate([before[k] for k in range(5)], 1)
    for i, y in enumerate(ys, 1):
        for copy in copies[i]:
            copy.wait()
        total += block_products(y[...], held, i)
    for copy in copies[0]:
        copy.wait()
    for k in range(5):
        out[k] = total[:, k * rank:(k + 1) * rank]


def block_products(y_here, held, i):
    dot = functools.partial(lax.dot_general, dimension_numbers=TN, preferred_element_type=jnp.float32)
    b_high, b_low = split(jnp.concatenate([held[i, 2], held[i, 3], held[i, 0], held[i, 1], y_here], 1))
    a_high, a_low = split(y_here)
    return dot(a_high, b_high) + dot(a_high, b_low) + dot(a_low, b_high)


def z_own_kernel(left, left_other, y, out, held, sems):
    rank = out.shape[-1]
    for copy in start_rows(left, left_other, held, sems, 1, y.shape[0])[0]:
        copy.wait()
    total = block_products(y[...], held, 0)
    for k in range(5):
        out[k] = total[:, k * rank:(k + 1) * rank]


def w_kernel(planes, sent, got, both, both_other, own, near, inner, inner_far, outer, last, *rest):
    *outs, held, sems = rest
    plane = lax.axis_index("tile")
    chip = lax.axis_index("step") // 2
    is_end = jnp.logical_or(plane == 0, plane == planes - 1)

    def pick(i, wanted, source):
        @pl.when(wanted)
        def _():
            pltpu.make_async_copy(source, held.at[i], sems.at[i]).start()

    for i in range(planes):
        block = jnp.bitwise_xor(chip, i)
        apart = jnp.bitwise_xor(block, plane)
        pick(i, apart == 0, own)
        pick(i, apart == 1, near)
        pick(i, jnp.logical_and(apart == 2, is_end), outer)
        pick(i, jnp.logical_and(apart == 2, jnp.logical_not(is_end)), inner_far)
        pick(i, jnp.logical_and(apart == 3, is_end), last)
        pick(i, jnp.logical_and(apart == 3, jnp.logical_not(is_end)), inner)
    returned = []
    for k in range(2):
        returned.append(dot3(sent[2 + k] + got[k], both[2 + k], NN))
    for k in range(2):
        returned.append(dot3(sent[k] + got[2 + k], both_other[2 + k], NN))
    returned = jnp.concatenate(returned, 1)
    for i, out in enumerate(outs):
        pltpu.make_async_copy(own, held.at[i], sems.at[i]).wait()
        out[...] = dot3(jnp.concatenate([held[i, k] for k in range(4)], 1), returned, NT)


def basis_kernel(tile_rows, width, group, sent, got, y_rows, basis, inverse):
    rank = inverse.shape[0]
    left = (sent[4] + got[4]) * (1.0 / tile_rows)
    index = lax.broadcasted_iota(jnp.int32, (rank, rank), 0)
    right = (index == lax.broadcasted_iota(jnp.int32, (rank, rank), 1)).astype(jnp.float32)
    row_index = lax.broadcasted_iota(jnp.int32, (width, rank), 0)
    done = []
    for begin in range(0, rank, width):
        l, r = left[:width], right[:width]
        scale = jnp.zeros((width, rank), jnp.float32)
        for first in range(0, width, group):
            place = begin + first
            columns = [jnp.broadcast_to(l[:, place + c:place + c + 1], (width, rank)) for c in range(group)]
            for c in range(group):
                j = first + c
                pivot = columns[c][j:j + 1]
                scale = jnp.where(row_index == j, lax.rsqrt(pivot), scale)
                factor = jnp.where(row_index > j, columns[c] * (1.0 / pivot), 0.0)
                for d in range(c + 1, group):
                    columns[d] = columns[d] - factor * columns[d][j:j + 1]
                l, r = l - factor * l[j:j + 1], r - factor * r[j:j + 1]
        l, r = l * scale, r * scale
        done.append(r)
        if begin + width < rank:
            both = dot_full(l[:, begin + width:], jnp.concatenate([l, r], 1), TN)
            left, right = left[width:] - both[:, :rank], right[width:] - both[:, rank:]
    lower_inverse = jnp.concatenate(done, 0)
    inverse[...] = lower_inverse
    basis[...] = dot_full(y_rows[...], lower_inverse, NT)


def factor_kernel(tile_rows, a, b, c, d, inverse, factor):
    total = (a[...] + b[...] + c[...] + d[...]) * (1.0 / tile_rows)
    factor[...] = dot_full(total, inverse[...], NT)


def local_line(target_left, target_right, column_left, column_right, sketch, pattern):
    tile_rows, rank = target_left.shape[2:]
    planes = lax.axis_size("tile")
    chips = lax.axis_size("step") // 2
    plane = lax.axis_index("tile")
    core_bit = lax.axis_index("step") % 2
    chip = lax.axis_index("step") // 2
    row_count = tile_rows // (2 * chips)
    is_end = jnp.logical_or(plane == 0, plane == planes - 1)
    outer_pairs, inner_pairs = [(0, 1), (1, 0), (2, 3), (3, 2)], [(1, 2), (2, 1)]
    outward = [(1, 0), (2, 3)]

    def across(array, pairs):
        return lax.ppermute(array, "tile", pairs)

    near = across(column_right, outer_pairs)
    inner = across(column_right, inner_pairs)
    probes = mm("kbq,bp->kqp", column_left, sketch)
    probes = probes + across(probes, outer_pairs)
    near, inner = lax.optimization_barrier((near, inner))
    right_blocks = target_right.reshape(2, planes, -1, rank)

    def block(index):
        return take(right_blocks, index, 1)

    inner_far = across(near, inner_pairs)
    outer_rows = jnp.where(is_end, block(planes - 1 - plane), inner)
    outer = across(outer_rows, outer_pairs)
    part = (
        mm("kbr,kbq->krq", block(plane), column_right)
        + mm("kbr,kbq->krq", block(plane ^ 1), near)
        + mm("kbr,kbq->krq", block(jnp.where(is_end, plane, planes - 1 - plane)), inner)
    )
    _, probes_held = lax.optimization_barrier(((near, inner), probes))
    probes_far = exchange(probes_held, "tile", 2)
    (lent,) = call(functools.partial(lent_kernel, planes), [(2, rank, rank)], [inner_far, outer])
    (core,) = call(functools.partial(core_kernel, planes), [(2, rank, rank)], [part, target_right, inner_far, outer])
    lent = across(lent, outward)

    left_split = target_left.reshape(2, chips, 2, row_count, rank)
    left_other = exchange(take(left_split, 1 - core_bit, 2), "step", 1)
    col_split = column_left.reshape(2, 2, row_count, rank)
    col_half = jnp.concatenate([take(col_split, core_bit, 1), exchange(take(col_split, 1 - core_bit, 1), "step", 1)])
    _, col_held = lax.optimization_barrier((part, col_half))
    col_near = across(col_held, outer_pairs)
    col_inner = across(col_held, inner_pairs)
    (both,) = call(reduced_kernel, [(4, rank, rank)], [core, lent, probes, probes_far, pattern], "vvvvs")
    _, near_held, inner_held = lax.optimization_barrier((both, col_near, col_inner))
    col_inner_far = across(near_held, inner_pairs)
    col_outer = across(inner_held, outward)
    col_inner_far, col_outer = lax.optimization_barrier((col_inner_far, col_outer))
    both_other = exchange(both, "step", 1)
    rows_scratch = [pltpu.VMEM((chips, 4, row_count, rank), jnp.float32), pltpu.SemaphoreType.DMA((2 * chips,))]
    y_parts = call(y_kernel, [(row_count, rank)] * chips, [target_left, left_other, both, both_other], "aavv", rows_scratch)
    y_rows = y_parts[0]
    for bit in range(chips - 1, 0, -1):
        y_rows = y_rows + exchange(y_parts[bit], "step", 2 * bit)
    y_all = [y_rows] + [exchange(y_rows, "step", 2 * bit) for bit in range(1, chips)]
    col_last = across(col_inner_far, outward)
    (own_sent,) = call(z_own_kernel, [(5, rank, rank)], [target_left, left_other, y_rows], "aav", rows_scratch)
    (sent,) = call(z_kernel, [(5, rank, rank)], [target_left, left_other, *y_all[1:], own_sent], "aa" + "v" * chips, rows_scratch)
    got = exchange(sent, "step", 1)
    w_parts = call(
        functools.partial(w_kernel, planes),
        [(row_count, rank)] * planes,
        [sent, got, both, both_other, col_half, col_near, col_inner, col_inner_far, col_outer, col_last],
        "vvvvaaaaaa",
        [pltpu.VMEM((planes, 4, row_count, rank), jnp.float32), pltpu.SemaphoreType.DMA((planes,))],
    )
    w_got = [exchange(w_parts[bit], "step", 2 * bit) for bit in range(1, chips)]
    basis, inverse = call(
        functools.partial(basis_kernel, tile_rows, 32, 16), [(row_count, rank), (rank, rank)], [sent, got, y_rows], cost=10**9
    )
    (factor,) = call(functools.partial(factor_kernel, tile_rows), [(row_count, rank)], [w_parts[0], *w_got, inverse])
    return basis[None], factor[None]


def solution(mesh):
    line = mesh.shape["tile"] == 4 and mesh.shape["step"] == 8
    return jax.shard_map(
        local_line if line else local_general,
        mesh=mesh,
        in_specs=(
            P("step", "tile", None, None),
            P("step", "tile", None, None),
            P("step", "tile", None),
            P("step", "tile", None),
            P("tile", None),
            P("step", "tile"),
        ),
        out_specs=(P("tile", "step", None), P("tile", "step", None)),
        check_vma=False,
    )
```

```python
import functools

import jax
import jax.numpy as jnp
from jax import lax
from jax.experimental import pallas as pl
from jax.experimental.pallas import tpu as pltpu
from jax.sharding import PartitionSpec as P

HIGH = lax.Precision.HIGH


def mm(spec, *arrays):
    return jnp.einsum(spec, *arrays, precision=HIGH, preferred_element_type=jnp.float32)


def inverse_factor(gram):
    lower = jnp.linalg.cholesky(gram)
    eye = jnp.eye(gram.shape[-1], dtype=gram.dtype)
    return jax.scipy.linalg.solve_triangular(lower, eye, lower=True)


def exchange(array, axis, bit):
    return lax.ppermute(array, axis, [(i, i ^ bit) for i in range(lax.axis_size(axis))])


def take(array, index, axis):
    return lax.dynamic_index_in_dim(array, index, axis, keepdims=False)


def local_general(target_left, target_right, column_left, column_right, sketch, pattern):
    left, right = target_left[:, 0], target_right[:, 0]
    tile_rows = left.shape[1]
    probes = lax.psum(mm("kbq,bp->kqp", column_left, sketch), "tile")
    col_left = lax.all_gather(column_left, "tile", axis=1, tiled=True)
    col_right = lax.all_gather(column_right, "tile", axis=1, tiled=True)
    core = mm("kbr,kbq->krq", right, col_right) * pattern[:, 0].astype(jnp.float32)[:, None, None]
    reduced = mm("krq,kqp->krp", core, probes)
    sketched = lax.psum(mm("kbr,krp->bp", left, reduced), "step")
    inverse = inverse_factor(mm("bp,bq->pq", sketched, sketched) / tile_rows)
    row_count = tile_rows // lax.axis_size("step")
    rows = lax.dynamic_slice_in_dim(sketched, lax.axis_index("step") * row_count, row_count, 0)
    projected = mm("kbr,bp->krp", left, sketched)
    returned = mm("krq,krp->kqp", core, projected)
    partial = mm("kbq,kqp->bp", col_left, returned)
    factor = lax.psum_scatter(partial, "step", scatter_dimension=0, tiled=True) / tile_rows
    return mm("bp,qp->bq", rows, inverse)[None], mm("bp,qp->bq", factor, inverse)[None]


TN = (((0,), (0,)), ((), ()))
NN = (((1,), (0,)), ((), ()))
NT = (((1,), (1,)), ((), ()))


def split(array):
    high = array.astype(jnp.bfloat16)
    return high, (array - high.astype(jnp.float32)).astype(jnp.bfloat16)


def dot3(a, b, dims):
    a_high, a_low = split(a)
    b_high, b_low = split(b)
    axis = 1 - dims[0][1][0]
    width = b.shape[axis]
    dot = functools.partial(lax.dot_general, dimension_numbers=dims, preferred_element_type=jnp.float32)
    wide = dot(a_high, jnp.concatenate([b_high, b_low], axis))
    return wide[:, :width] + wide[:, width:] + dot(a_low, b_high)


def dot_full(a, b, dims):
    return lax.dot_general(a, b, dims, precision=lax.Precision.HIGHEST, preferred_element_type=jnp.float32)


def call(kernel, outs, args, spaces="", scratch=(), cost=0):
    kinds = {"v": pltpu.VMEM, "a": pl.ANY, "s": pltpu.SMEM}
    spaces = spaces or "v" * len(args)
    shapes = [jax.ShapeDtypeStruct(shape, jnp.float32) for shape in outs]
    return pl.pallas_call(
        kernel,
        out_shape=shapes,
        in_specs=[pl.BlockSpec(memory_space=kinds[letter]) for letter in spaces],
        out_specs=[pl.BlockSpec(memory_space=pltpu.VMEM) for _ in shapes],
        scratch_shapes=list(scratch),
        compiler_params=pltpu.CompilerParams(vmem_limit_bytes=24 << 20),
        cost_estimate=pl.CostEstimate(flops=cost, bytes_accessed=0, transcendentals=0),
    )(*args)


def lent_kernel(planes, first, second, lent):
    plane = lax.axis_index("tile")
    is_end = jnp.logical_or(plane == 0, plane == planes - 1)

    @pl.when(is_end)
    def _():
        for k in range(2):
            lent[k] = jnp.zeros(lent.shape[1:], jnp.float32)

    @pl.when(jnp.logical_not(is_end))
    def _():
        for k in range(2):
            lent[k] = dot3(second[k], first[k], TN)


def core_kernel(planes, part, right, first, second, core):
    plane = lax.axis_index("tile")
    rows = first.shape[1]
    far = pl.ds(pl.multiple_of(jnp.bitwise_xor(plane, 2) * rows, rows), rows)
    is_end = jnp.logical_or(plane == 0, plane == planes - 1)

    @pl.when(is_end)
    def _():
        for k in range(2):
            core[k] = part[k] + dot3(right[k, 0, far, :], second[k], TN)

    @pl.when(jnp.logical_not(is_end))
    def _():
        for k in range(2):
            core[k] = part[k] + dot3(right[k, 0, far, :], first[k], TN)


def reduced_kernel(core, lent, probe_here, probe_far, pattern, both):
    for k in range(2):
        weight = pattern[k, 0].astype(jnp.float32)
        c = (core[k] + lent[k]) * weight
        both[k] = dot3(c, probe_here[k] + probe_far[k], NN)
        both[2 + k] = c


def start_rows(left, left_other, held, sems, chips, rows):
    position = lax.axis_index("step")
    chip, bit = position // 2, position % 2
    copies = []
    for i in range(chips):
        block = jnp.bitwise_xor(chip, i)
        pair = [None, None]
        if left is not None:
            mine = left.at[:, 0, pl.ds(pl.multiple_of((block * 2 + bit) * rows, rows), rows), :]
            pair[0] = pltpu.make_async_copy(mine, held.at[i, pl.ds(0, 2)], sems.at[2 * i])
        if left_other is not None:
            pair[1] = pltpu.make_async_copy(left_other.at[:, block], held.at[i, pl.ds(2, 2)], sems.at[2 * i + 1])
        copies.append(pair)
    for pair in copies:
        for copy in pair:
            if copy is not None:
                copy.start()
    return copies


def y_own_kernel(left, both, *rest):
    *outs, held, sems = rest
    chips, rows = len(outs), outs[0].shape[0]
    copies = [pair[0] for pair in start_rows(left, None, held, sems, chips, rows)]
    reduced = jnp.concatenate([both[0], both[1]], 0)
    for i, out in enumerate(outs):
        copies[i].wait()
        out[...] = dot3(jnp.concatenate([held[i, 0], held[i, 1]], 1), reduced, NN)


def y_kernel(left_other, both_other, *rest):
    *blocks, held, sems = rest
    chips = len(blocks) // 2
    rows = blocks[0].shape[0]
    copies = [pair[1] for pair in start_rows(None, left_other, held, sems, chips, rows)]
    reduced = jnp.concatenate([both_other[0], both_other[1]], 0)
    for i in range(chips):
        copies[i].wait()
        blocks[chips + i][...] = blocks[i][...] + dot3(jnp.concatenate([held[i, 2], held[i, 3]], 1), reduced, NN)


def z_kernel(left, left_other, *rest):
    *ys, before, out, held, sems = rest
    rows = ys[0].shape[0]
    rank = out.shape[-1]
    copies = start_rows(left, left_other, held, sems, len(ys) + 1, rows)
    total = jnp.concatenate([before[k] for k in range(5)], 1)
    for i, y in enumerate(ys, 1):
        for copy in copies[i]:
            copy.wait()
        total += block_products(y[...], held, i)
    for copy in copies[0]:
        copy.wait()
    for k in range(5):
        out[k] = total[:, k * rank:(k + 1) * rank]


def block_products(y_here, held, i):
    dot = functools.partial(lax.dot_general, dimension_numbers=TN, preferred_element_type=jnp.float32)
    b_high, b_low = split(jnp.concatenate([held[i, 2], held[i, 3], held[i, 0], held[i, 1], y_here], 1))
    a_high, a_low = split(y_here)
    return dot(a_high, b_high) + dot(a_high, b_low) + dot(a_low, b_high)


def z_own_kernel(left, left_other, y, out, held, sems):
    rank = out.shape[-1]
    for copy in start_rows(left, left_other, held, sems, 1, y.shape[0])[0]:
        copy.wait()
    total = block_products(y[...], held, 0)
    for k in range(5):
        out[k] = total[:, k * rank:(k + 1) * rank]


def w_kernel(planes, sent, got, both, both_other, own, near, inner, inner_far, outer, last, *rest):
    *outs, held, sems = rest
    plane = lax.axis_index("tile")
    chip = lax.axis_index("step") // 2
    is_end = jnp.logical_or(plane == 0, plane == planes - 1)

    def pick(i, wanted, source):
        @pl.when(wanted)
        def _():
            pltpu.make_async_copy(source, held.at[i], sems.at[i]).start()

    for i in range(planes):
        block = jnp.bitwise_xor(chip, i)
        apart = jnp.bitwise_xor(block, plane)
        pick(i, apart == 0, own)
        pick(i, apart == 1, near)
        pick(i, jnp.logical_and(apart == 2, is_end), outer)
        pick(i, jnp.logical_and(apart == 2, jnp.logical_not(is_end)), inner_far)
        pick(i, jnp.logical_and(apart == 3, is_end), last)
        pick(i, jnp.logical_and(apart == 3, jnp.logical_not(is_end)), inner)
    returned = []
    for k in range(2):
        returned.append(dot3(sent[2 + k] + got[k], both[2 + k], NN))
    for k in range(2):
        returned.append(dot3(sent[k] + got[2 + k], both_other[2 + k], NN))
    returned = jnp.concatenate(returned, 1)
    for i, out in enumerate(outs):
        pltpu.make_async_copy(own, held.at[i], sems.at[i]).wait()
        out[...] = dot3(jnp.concatenate([held[i, k] for k in range(4)], 1), returned, NT)


def basis_kernel(tile_rows, width, group, sent, got, y_rows, basis, inverse):
    rank = inverse.shape[0]
    left = (sent[4] + got[4]) * (1.0 / tile_rows)
    index = lax.broadcasted_iota(jnp.int32, (rank, rank), 0)
    right = (index == lax.broadcasted_iota(jnp.int32, (rank, rank), 1)).astype(jnp.float32)
    row_index = lax.broadcasted_iota(jnp.int32, (width, rank), 0)
    done = []
    for begin in range(0, rank, width):
        l, r = left[:width], right[:width]
        scale = jnp.zeros((width, rank), jnp.float32)
        for first in range(0, width, group):
            place = begin + first
            columns = [jnp.broadcast_to(l[:, place + c:place + c + 1], (width, rank)) for c in range(group)]
            for c in range(group):
                j = first + c
                pivot = columns[c][j:j + 1]
                scale = jnp.where(row_index == j, lax.rsqrt(pivot), scale)
                factor = jnp.where(row_index > j, columns[c] * (1.0 / pivot), 0.0)
                for d in range(c + 1, group):
                    columns[d] = columns[d] - factor * columns[d][j:j + 1]
                l, r = l - factor * l[j:j + 1], r - factor * r[j:j + 1]
        l, r = l * scale, r * scale
        done.append(r)
        if begin + width < rank:
            both = dot_full(l[:, begin + width:], jnp.concatenate([l, r], 1), TN)
            left, right = left[width:] - both[:, :rank], right[width:] - both[:, rank:]
    lower_inverse = jnp.concatenate(done, 0)
    inverse[...] = lower_inverse
    basis[...] = dot_full(y_rows[...], lower_inverse, NT)


def factor_kernel(tile_rows, a, b, c, d, inverse, factor):
    total = (a[...] + b[...] + c[...] + d[...]) * (1.0 / tile_rows)
    factor[...] = dot_full(total, inverse[...], NT)


def local_line(target_left, target_right, column_left, column_right, sketch, pattern):
    tile_rows, rank = target_left.shape[2:]
    planes = lax.axis_size("tile")
    chips = lax.axis_size("step") // 2
    plane = lax.axis_index("tile")
    core_bit = lax.axis_index("step") % 2
    chip = lax.axis_index("step") // 2
    row_count = tile_rows // (2 * chips)
    is_end = jnp.logical_or(plane == 0, plane == planes - 1)
    outer_pairs, inner_pairs = [(0, 1), (1, 0), (2, 3), (3, 2)], [(1, 2), (2, 1)]
    outward = [(1, 0), (2, 3)]

    def across(array, pairs):
        return lax.ppermute(array, "tile", pairs)

    near = across(column_right, outer_pairs)
    inner = across(column_right, inner_pairs)
    probes = mm("kbq,bp->kqp", column_left, sketch)
    probes = probes + across(probes, outer_pairs)
    near, inner = lax.optimization_barrier((near, inner))
    right_blocks = target_right.reshape(2, planes, -1, rank)

    def block(index):
        return take(right_blocks, index, 1)

    inner_far = across(near, inner_pairs)
    outer_rows = jnp.where(is_end, block(planes - 1 - plane), inner)
    outer = across(outer_rows, outer_pairs)
    part = (
        mm("kbr,kbq->krq", block(plane), column_right)
        + mm("kbr,kbq->krq", block(plane ^ 1), near)
        + mm("kbr,kbq->krq", block(jnp.where(is_end, plane, planes - 1 - plane)), inner)
    )
    _, probes_held = lax.optimization_barrier(((near, inner), probes))
    probes_far = exchange(probes_held, "tile", 2)
    (lent,) = call(functools.partial(lent_kernel, planes), [(2, rank, rank)], [inner_far, outer])
    (core,) = call(functools.partial(core_kernel, planes), [(2, rank, rank)], [part, target_right, inner_far, outer])
    lent = across(lent, outward)

    left_split = target_left.reshape(2, chips, 2, row_count, rank)
    left_other = exchange(take(left_split, 1 - core_bit, 2), "step", 1)
    col_split = column_left.reshape(2, 2, row_count, rank)
    col_half = jnp.concatenate([take(col_split, core_bit, 1), exchange(take(col_split, 1 - core_bit, 1), "step", 1)])
    _, col_held = lax.optimization_barrier((part, col_half))
    col_near = across(col_held, outer_pairs)
    col_inner = across(col_held, inner_pairs)
    (both,) = call(reduced_kernel, [(4, rank, rank)], [core, lent, probes, probes_far, pattern], "vvvvs")
    _, near_held, inner_held = lax.optimization_barrier((both, col_near, col_inner))
    col_inner_far = across(near_held, inner_pairs)
    col_outer = across(inner_held, outward)
    col_inner_far, col_outer = lax.optimization_barrier((col_inner_far, col_outer))
    both_other = exchange(both, "step", 1)
    rows_scratch = [pltpu.VMEM((chips, 4, row_count, rank), jnp.float32), pltpu.SemaphoreType.DMA((2 * chips,))]
    y_own = call(y_own_kernel, [(row_count, rank)] * chips, [target_left, both], "av", rows_scratch)
    y_parts = call(y_kernel, [(row_count, rank)] * chips, [left_other, both_other, *y_own], "av" + "v" * chips, rows_scratch)
    y_rows = y_parts[0]
    for bit in range(chips - 1, 0, -1):
        y_rows = y_rows + exchange(y_parts[bit], "step", 2 * bit)
    y_all = [y_rows] + [exchange(y_rows, "step", 2 * bit) for bit in range(1, chips)]
    col_last = across(col_inner_far, outward)
    (own_sent,) = call(z_own_kernel, [(5, rank, rank)], [target_left, left_other, y_rows], "aav", rows_scratch)
    (sent,) = call(z_kernel, [(5, rank, rank)], [target_left, left_other, *y_all[1:], own_sent], "aa" + "v" * chips, rows_scratch)
    got = exchange(sent, "step", 1)
    w_parts = call(
        functools.partial(w_kernel, planes),
        [(row_count, rank)] * planes,
        [sent, got, both, both_other, col_half, col_near, col_inner, col_inner_far, col_outer, col_last],
        "vvvvaaaaaa",
        [pltpu.VMEM((planes, 4, row_count, rank), jnp.float32), pltpu.SemaphoreType.DMA((planes,))],
    )
    w_got = [exchange(w_parts[bit], "step", 2 * bit) for bit in range(1, chips)]
    basis, inverse = call(
        functools.partial(basis_kernel, tile_rows, 32, 16), [(row_count, rank), (rank, rank)], [sent, got, y_rows], cost=10**9
    )
    (factor,) = call(functools.partial(factor_kernel, tile_rows), [(row_count, rank)], [w_parts[0], *w_got, inverse])
    return basis[None], factor[None]


def solution(mesh):
    line = mesh.shape["tile"] == 4 and mesh.shape["step"] == 8
    return jax.shard_map(
        local_line if line else local_general,
        mesh=mesh,
        in_specs=(
            P("step", "tile", None, None),
            P("step", "tile", None, None),
            P("step", "tile", None),
            P("step", "tile", None),
            P("tile", None),
            P("step", "tile"),
        ),
        out_specs=(P("tile", "step", None), P("tile", "step", None)),
        check_vma=False,
    )
```
